128 devices in a mesh: photo: 4 (over y), worker: 32 (over x, z, core).
Axes of the slice: x: 4, y: 4, z: 4, core: 2. Of those that a mesh axis runs over, the one named last changes fastest.
Arguments:
- descriptors: bfloat16 [512, 1024, 256], P(('photo', 'worker'))
- key_counts: int32 [512], replicated, may hold values from 256 to 1024
- pair_list: int32 [512, 2], P(('photo', 'worker')), may hold values from 0 to 511, as said below
- w_qk: bfloat16 [256, 256], replicated, may hold values from -0.375 to 0.375
- w_value: bfloat16 [256, 256], replicated, may hold values from -0.375 to 0.375
- w_out: bfloat16 [256, 256], replicated, may hold values from -0.375 to 0.375
- w_up: bfloat16 [512, 512], replicated, may hold values from -0.25 to 0.25
- b_up: float32 [512], replicated, may hold values from -3 to 3
- ln_gain: float32 [512], replicated, may hold values from 0.5 to 1.5
- ln_bias: float32 [512], replicated, may hold values from -3 to 3
- w_down: bfloat16 [512, 256], replicated, may hold values from -0.25 to 0.25
- b_down: float32 [256], replicated, may hold values from -3 to 3
Outputs:
- pair_states: bfloat16 [512, 2, 1024, 256], P(('photo', 'worker'))
- pooled_update: float32 [512, 1024, 256], P(('photo', 'worker'))
The draws below stay inside these ranges and needn't reach their ends.
Inputs may be any that keep to these rules, and one draw needn't show every extreme that they name: `pair_list`: on pair p the first image is (p // 4) * 4 + p % 4; the second is a different image whose index divided by 4 differs from that of the first by at most one, and both differences of one occur.
All inputs are finite; a program needn't handle non-finite values.
Results may differ from the reference program's by a relative error of at most 0.007.
Values may be sent and summed in bfloat16 or wider, within the bound.
A program may use at most 128 MiB of HBM per device.

```python
import jax
import jax.numpy as jnp
from jax import lax

D = 256
HEAD_DIM = 64
MLP_WIDTH = 512
K = 1024
IMG_DEV = 4
PAIR_DEV = 4
IMAGES = 512
PAIRS = 512


def draw_descriptors(key, part):
    keys = jax.random.split(jax.random.fold_in(key, 37), 5)
    devices_all = IMAGES // IMG_DEV
    pool = max(K // 4, 1)
    landmarks = jnp.clip(jax.random.normal(keys[0], (devices_all, pool, D), jnp.float32), -6.0, 6.0)
    fresh = jnp.clip(jax.random.normal(keys[1], (IMAGES, K, D), jnp.float32), -6.0, 6.0)
    owner = jnp.arange(IMAGES, dtype=jnp.int32) // IMG_DEV
    side = jax.random.randint(keys[2], (IMAGES, K), -1, 2)
    source = jnp.clip(owner[:, None] + side, 0, devices_all - 1)
    landmark_slot = jax.random.randint(keys[3], (IMAGES, K), 0, pool)
    copied = landmarks[source, landmark_slot] + 0.3 * fresh
    keep = jax.random.randint(keys[4], (IMAGES, K), 0, 5) < 3
    values = jnp.where(keep[:, :, None], copied, fresh)
    return values.astype(jnp.bfloat16)


def draw_key_counts(key, part):
    first_key, second_key, third_key = jax.random.split(jax.random.fold_in(key, 11), 3)
    counts = jax.random.randint(first_key, (IMAGES,), K // 4, K + 1)
    top_place = jax.random.randint(second_key, (), 0, IMAGES)
    low_place = (top_place + 1 + jax.random.randint(third_key, (), 0, IMAGES - 1)) % IMAGES
    counts = counts.at[top_place].set(K)
    counts = counts.at[low_place].set(K // 4)
    return counts.astype(jnp.int32)


def draw_pair_list(key, part):
    first_key, second_key, third_key = jax.random.split(jax.random.fold_in(key, 23), 3)
    devices_all = PAIRS // PAIR_DEV
    index = jnp.arange(PAIRS, dtype=jnp.int32)
    device = index // PAIR_DEV
    slot = index % PAIR_DEV
    owned = device * IMG_DEV + slot % IMG_DEV
    drift = jax.random.randint(first_key, (PAIRS,), -1, 2)
    side = jnp.where(slot == 0, 1, jnp.where(slot == 1, -1, drift))
    side = jnp.where(device + side > devices_all - 1, -1, side)
    side = jnp.where(device + side < 0, 1, side)
    partner = (device + side) * IMG_DEV + jax.random.randint(second_key, (PAIRS,), 0, IMG_DEV)
    other_local = (slot % IMG_DEV + 1 + jax.random.randint(third_key, (PAIRS,), 0, IMG_DEV - 1)) % IMG_DEV
    partner = jnp.where(side == 0, device * IMG_DEV + other_local, partner)
    return jnp.stack([owned, partner], axis=-1).astype(jnp.int32)


def bell_draw(key, extent, deviation, bound, held_as=jnp.bfloat16):
    array = jax.random.normal(key, extent, jnp.float32) * deviation
    return jnp.minimum(jnp.maximum(array, -bound), bound).astype(held_as)


def setup_inputs(seed: int = 0) -> dict:
    seeds = jax.random.split(jax.random.key(seed), 13)
    descriptors = draw_descriptors(jax.random.fold_in(seeds[12], 71), 0)
    key_counts = draw_key_counts(jax.random.fold_in(seeds[12], 71), 0)
    pair_list = draw_pair_list(jax.random.fold_in(seeds[12], 71), 0)
    w_qk = bell_draw(seeds[3], (D, D), D ** -0.5, 0.375)
    w_value = bell_draw(seeds[4], (D, D), D ** -0.5, 0.375)
    w_out = bell_draw(seeds[5], (D, D), D ** -0.5, 0.375)
    w_up = bell_draw(seeds[6], (MLP_WIDTH, MLP_WIDTH), MLP_WIDTH ** -0.5, 0.25)
    b_up = bell_draw(seeds[7], (MLP_WIDTH,), 0.5, 3.0, jnp.float32)
    ln_gain = jnp.clip(1.0 + 0.1 * jax.random.normal(seeds[8], (MLP_WIDTH,), jnp.float32), 0.5, 1.5)
    ln_bias = bell_draw(seeds[9], (MLP_WIDTH,), 0.5, 3.0, jnp.float32)
    w_down = bell_draw(seeds[10], (MLP_WIDTH, D), MLP_WIDTH ** -0.5, 0.25)
    b_down = bell_draw(seeds[11], (D,), 0.5, 3.0, jnp.float32)
    return dict(descriptors=descriptors, key_counts=key_counts, pair_list=pair_list, w_qk=w_qk, w_value=w_value, w_out=w_out, w_up=w_up, b_up=b_up, ln_gain=ln_gain, ln_bias=ln_bias, w_down=w_down, b_down=b_down)


def attend(queries, keys, values, count):
    heads = queries.shape[1] // HEAD_DIM
    query_heads = queries.astype(jnp.float32).reshape(K, heads, HEAD_DIM)
    key_heads = keys.astype(jnp.float32).reshape(K, heads, HEAD_DIM)
    value_heads = values.astype(jnp.float32).reshape(K, heads, HEAD_DIM)
    scores = jnp.einsum('qhd,khd->hqk', query_heads, key_heads) * HEAD_DIM ** (-0.5)
    valid = jnp.arange(K, dtype=jnp.int32) < count
    scores = jnp.where(valid[None, None, :], scores, -jnp.inf)
    weights = jax.nn.softmax(scores, axis=-1).astype(jnp.bfloat16).astype(jnp.float32)
    mixed = jnp.einsum('hqk,khd->qhd', weights, value_heads)
    return mixed.reshape(K, heads * HEAD_DIM).astype(jnp.bfloat16)

def refine(start, message, w_out, w_up, b_up, ln_gain, ln_bias, w_down, b_down):
    sent = jnp.dot(message, w_out, preferred_element_type=jnp.float32).astype(jnp.bfloat16)
    joined = jnp.concatenate([start, sent], axis=-1)
    hidden = jnp.dot(joined, w_up, preferred_element_type=jnp.float32) + b_up
    center = lax.optimization_barrier(jnp.mean(hidden, axis=-1, keepdims=True))
    spread = lax.optimization_barrier(jnp.mean((hidden - center) ** 2, axis=-1, keepdims=True))
    normed = (hidden - center) * lax.rsqrt(spread + 1e-05) * ln_gain + ln_bias
    act = jax.nn.gelu(normed, approximate=False).astype(jnp.bfloat16)
    delta = jnp.dot(act, w_down, preferred_element_type=jnp.float32) + b_down
    return ((start.astype(jnp.float32) + delta).astype(jnp.bfloat16), delta)

def reference(descriptors, key_counts, pair_list, w_qk, w_value, w_out, w_up, b_up, ln_gain, ln_bias, w_down, b_down):

    def step(pooled, pair_row):
        first = pair_row[0].astype(jnp.int32)
        second = pair_row[1].astype(jnp.int32)
        x_first = lax.dynamic_index_in_dim(descriptors, first, 0, keepdims=False)
        x_second = lax.dynamic_index_in_dim(descriptors, second, 0, keepdims=False)
        count_first = lax.dynamic_index_in_dim(key_counts, first, 0, keepdims=False)
        count_second = lax.dynamic_index_in_dim(key_counts, second, 0, keepdims=False)
        qk_first = jnp.dot(x_first, w_qk, preferred_element_type=jnp.float32).astype(jnp.bfloat16)
        qk_second = jnp.dot(x_second, w_qk, preferred_element_type=jnp.float32).astype(jnp.bfloat16)
        val_first = jnp.dot(x_first, w_value, preferred_element_type=jnp.float32).astype(jnp.bfloat16)
        val_second = jnp.dot(x_second, w_value, preferred_element_type=jnp.float32).astype(jnp.bfloat16)
        msg_first = attend(qk_first, qk_second, val_second, count_second)
        msg_second = attend(qk_second, qk_first, val_first, count_first)
        new_first, delta_first = refine(x_first, msg_first, w_out, w_up, b_up, ln_gain, ln_bias, w_down, b_down)
        new_second, delta_second = refine(x_second, msg_second, w_out, w_up, b_up, ln_gain, ln_bias, w_down, b_down)
        pooled = pooled.at[first].add(delta_first)
        pooled = pooled.at[second].add(delta_second)
        return (pooled, jnp.stack([new_first, new_second], axis=0))
    pooled0 = jnp.zeros((IMAGES, K, D), jnp.float32)
    pooled, pair_states = lax.scan(step, pooled0, pair_list)
    return (pair_states, pooled)
```

```python
import functools
import jax
import jax.numpy as jnp
from jax import lax
from jax.experimental import pallas as pl
from jax.experimental.pallas import tpu as pltpu
from jax.sharding import PartitionSpec as P

K = 1024
D = 256
HEADS = 4
HEAD_DIM = 64
ROWS = 256
BF = jnp.bfloat16
F32 = jnp.float32


def dg(a, b, ca, cb):
    return lax.dot_general(a, b, (((ca,), (cb,)), ((), ())), preferred_element_type=F32)


def lane(shape):
    return lax.broadcasted_iota(jnp.int32, shape, 1)


def row(shape):
    return lax.broadcasted_iota(jnp.int32, shape, 0)


def project(xa, xb, ca, cb, wqk, wval, wvalt, qm, kb, vext, vtext):
    qa = dg(xa[...], wqk[...], 1, 0).astype(BF)
    kb[...] = dg(xb[...], wqk[...], 1, 0).astype(BF)
    qs = qa * jnp.asarray(HEAD_DIM**-0.5, BF)
    lanes = lane((K, D))
    for h in range(HEADS):
        inside = (lanes >= h * HEAD_DIM) & (lanes < (h + 1) * HEAD_DIM)
        qm[h] = jnp.where(inside, qs, jnp.zeros_like(qs))
    vb = dg(xb[...], wval[...], 1, 0)
    half = lane((K, 128)) < HEAD_DIM
    valid = row((K, 128)) < cb
    for h in range(HEADS):
        part = vb[:, 128 * (h // 2) : 128 * (h // 2 + 1)]
        keep = half if h % 2 == 0 else jnp.logical_not(half)
        vext[h] = jnp.where(valid, jnp.where(keep, part, 1.0), 0.0).astype(BF)
    vat = dg(wvalt[...], xa[...], 1, 1)
    validt = lane((D, K)) < ca
    vat = jnp.where(validt, vat, 0.0).astype(BF)
    ones = jnp.where(lane((HEAD_DIM, K)) < ca, 1.0, 0.0).astype(BF)
    for h in range(HEADS):
        vtext[h, :HEAD_DIM] = vat[h * HEAD_DIM : (h + 1) * HEAD_DIM]
        vtext[h, HEAD_DIM:] = ones


def attention(qm, kb, vext, vtext, e, ma, mbt):
    half = lane((ROWS, 128)) < HEAD_DIM
    for g in range(HEADS // 2):
        us = []
        for h in (2 * g, 2 * g + 1):
            slot = h % 2
            for ib in range(K // ROWS):
                rows = slice(ib * ROWS, (ib + 1) * ROWS)
                s = dg(qm[h, rows], kb[...], 1, 1)
                p = jnp.exp(s).astype(BF)
                e[slot, rows] = p
                u = dg(p, vext[h], 1, 0)
                n = u / pltpu.roll(u, HEAD_DIM, 1)
                cols = slice(128 * g, 128 * (g + 1))
                if slot == 0:
                    ma[rows, cols] = n.astype(BF)
                else:
                    ma[rows, cols] = jnp.where(half, ma[rows, cols], n.astype(BF))
            ut = dg(vtext[h], e[slot], 1, 0)
            mbt[h * HEAD_DIM : (h + 1) * HEAD_DIM] = (ut[:HEAD_DIM] / ut[HEAD_DIM:]).astype(BF)


def mlp(x, m, wout, wup, bup, gain, bias, wdown, bdown):
    sent = dg(m, wout[...], 1, 0).astype(BF)
    hidden = dg(x, wup[:D], 1, 0) + dg(sent, wup[D:], 1, 0) + bup[...]
    center = jnp.mean(hidden, axis=-1, keepdims=True)
    c = hidden - center
    spread = jnp.mean(c * c, axis=-1, keepdims=True)
    normed = c * lax.rsqrt(spread + 1e-05) * gain[...] + bias[...]
    act = (0.5 * normed * (1.0 + lax.erf(normed * 0.7071067811865476))).astype(BF)
    return dg(act, wdown[...], 1, 0) + bdown[...]


def attend_shifted(qm, kb, vext, vtext, cb, ca, ma, mbt):
    blocks = K // ROWS

    def step(index, _):
        h = index // blocks
        start = pl.multiple_of((index % blocks) * ROWS, ROWS)
        rows = pl.ds(start, ROWS)
        column = lane((ROWS, K))
        s = jnp.where(column < cb, dg(qm[h, rows], kb[...], 1, 1), -jnp.inf)
        p = jnp.exp(s - jnp.max(s, axis=-1, keepdims=True)).astype(BF)
        u = dg(p, vext[h], 1, 0)
        n = (u / pltpu.roll(u, HEAD_DIM, 1)).astype(BF)
        left = lane((ROWS, 128)) < HEAD_DIM
        for g in range(HEADS // 2):
            cols = slice(128 * g, 128 * (g + 1))
            mine = left & (h == 2 * g) | jnp.logical_not(left) & (h == 2 * g + 1)
            ma[rows, cols] = jnp.where(mine, n, ma[rows, cols])
        s = jnp.where(column < ca, dg(kb[rows], qm[h], 1, 1), -jnp.inf)
        p = jnp.exp(s - jnp.max(s, axis=-1, keepdims=True)).astype(BF)
        ut = dg(vtext[h], p, 1, 1)
        out = pl.ds(pl.multiple_of(h * HEAD_DIM, HEAD_DIM), HEAD_DIM)
        mbt[out, rows] = (ut[:HEAD_DIM] / ut[HEAD_DIM:]).astype(BF)
        return 0

    ma[...] = jnp.zeros_like(ma)
    lax.fori_loop(0, HEADS * blocks, step, 0)


def widest(qk, heads):
    square = qk.astype(F32) * qk.astype(F32)
    return jnp.max(dg(square.astype(BF), heads, 1, 0))


def pairs_kernel(p0, plist, counts, base, xa, before, own, after, wqk, wval, wvalt, wout, wup, bup, gain,
                 bias, wdown, bdown, *rest):
    (states, da, db, xb, qm, kb, vext, vtext, e, ma, mbt, sem) = rest[-12:]
    p = p0 + pl.program_id(0)
    first, second = plist[2 * p], plist[2 * p + 1]
    ca, cb = counts[first], counts[second]
    place = second - base[0]

    for low, source in ((-4, before), (0, own), (4, after)):

        @pl.when((place >= low) & (place < low + 4))
        def _():
            copy = pltpu.make_async_copy(source.at[place - low], xb, sem)
            copy.start()
            copy.wait()

    x = xa.at[0]
    project(x, xb, ca, cb, wqk, wval, wvalt, qm, kb, vext, vtext)
    heads = jnp.where(row((D, 128)) // HEAD_DIM == lane((D, 128)), 1.0, 0.0).astype(BF)
    qa = qm[0] + qm[1] + qm[2] + qm[3]
    bound = widest(qa, heads) * widest(kb[...], heads)
    tall = jnp.maximum(jnp.max(jnp.abs(vext[...].astype(F32))), jnp.max(jnp.abs(vtext[...].astype(F32))))
    narrow = (bound < 60.0 * 60.0) & (tall < 1e9)

    @pl.when(narrow)
    def _():
        attention(qm, kb, vext, vtext, e, ma, mbt)

    @pl.when(jnp.logical_not(narrow))
    def _():
        attend_shifted(qm, kb, vext, vtext, cb, ca, ma, mbt)

    weights = (wout, wup, bup, gain, bias, wdown, bdown)
    for ib in range(K // ROWS):
        rows = slice(ib * ROWS, (ib + 1) * ROWS)
        delta = mlp(xb[rows], mbt[:, rows].T, *weights)
        states[0, 1, rows] = (xb[rows].astype(F32) + delta).astype(BF)
        db[0, rows] = delta.astype(BF)
    for ib in range(K // ROWS):
        rows = slice(ib * ROWS, (ib + 1) * ROWS)
        delta = mlp(x[rows], ma[rows], *weights)
        states[0, 0, rows] = (x[rows].astype(F32) + delta).astype(BF)
        da[0, rows] = delta


def pool_kernel(mine, lower, upper, base, da, own1, own2, low1, low2, up1, up2, out):
    g = pl.program_id(0)
    image = base[0] + g
    out[0] = da[0]
    for plist, parts in ((mine, (own1, own2)), (lower, (low1, low2)), (upper, (up1, up2))):
        for p in range(4):

            @pl.when(plist[2 * p + 1] == image)
            def _():
                out[0] += parts[p // 2][p % 2].astype(F32)


AXES = ("photo", "worker")


def local(descriptors, key_counts, pair_list, w_qk, w_value, w_out, w_up, b_up, ln_gain, ln_bias, w_down, b_down):
    peers = lax.axis_size(AXES)
    up = [(i, (i + 1) % peers) for i in range(peers)]
    down = [(j, i) for i, j in up]
    flat = pair_list.reshape(-1)
    before = lax.ppermute(descriptors, AXES, up)
    after = lax.ppermute(descriptors, AXES, down)
    lower_list = lax.ppermute(flat, AXES, up)
    upper_list = lax.ppermute(flat, AXES, down)
    base = (lax.axis_index(AXES) * 4).astype(jnp.int32).reshape(1)
    whole = pl.BlockSpec(memory_space=pltpu.VMEM)
    smem = pl.BlockSpec(memory_space=pltpu.SMEM)
    hbm = pl.BlockSpec(memory_space=pl.ANY)
    weights = (w_qk, w_value, w_value.T, w_out, w_up, b_up[None], ln_gain[None], ln_bias[None], w_down, b_down[None])

    def pairs(p0, aliased):
        n_in = 7 + len(weights)
        return pl.pallas_call(
            functools.partial(pairs_kernel, p0),
            grid=(2,),
            out_shape=(
                jax.ShapeDtypeStruct((4, 2, K, D), BF),
                jax.ShapeDtypeStruct((4, K, D), F32),
                jax.ShapeDtypeStruct((2, K, D), BF),
            ),
            in_specs=[smem] * 3
            + [pl.BlockSpec((1, K, D), lambda i: (p0 + i, 0, 0)), hbm, hbm, hbm]
            + [whole] * len(weights)
            + [hbm] * len(aliased),
            out_specs=(
                pl.BlockSpec((1, 2, K, D), lambda i: (p0 + i, 0, 0, 0)),
                pl.BlockSpec((1, K, D), lambda i: (p0 + i, 0, 0)),
                pl.BlockSpec((1, K, D), lambda i: (i, 0, 0)),
            ),
            scratch_shapes=[
                pltpu.VMEM((K, D), BF),
                pltpu.VMEM((HEADS, K, D), BF),
                pltpu.VMEM((K, D), BF),
                pltpu.VMEM((HEADS, K, 128), BF),
                pltpu.VMEM((HEADS, 128, K), BF),
                pltpu.VMEM((2, K, K), BF),
                pltpu.VMEM((K, D), BF),
                pltpu.VMEM((D, K), BF),
                pltpu.SemaphoreType.DMA,
            ],
            input_output_aliases={n_in: 0, n_in + 1: 1} if aliased else {},
            compiler_params=pltpu.CompilerParams(vmem_limit_bytes=50 * 2**20),
            cost_estimate=pl.CostEstimate(flops=20 * 10**9, bytes_accessed=10**7, transcendentals=0),
        )(flat, key_counts, base, descriptors, before, descriptors, after, *weights, *aliased)

    states, terms, part1 = pairs(0, ())
    low1 = lax.ppermute(part1, AXES, up)
    up1 = lax.ppermute(part1, AXES, down)
    states, terms, part2 = pairs(2, (states, terms))
    low2 = lax.ppermute(part2, AXES, up)
    up2 = lax.ppermute(part2, AXES, down)
    pooled = pl.pallas_call(
        pool_kernel,
        grid=(4,),
        out_shape=jax.ShapeDtypeStruct((4, K, D), F32),
        in_specs=[smem] * 4 + [pl.BlockSpec((1, K, D), lambda i: (i, 0, 0))] + [whole] * 6,
        out_specs=pl.BlockSpec((1, K, D), lambda i: (i, 0, 0)),
        compiler_params=pltpu.CompilerParams(vmem_limit_bytes=50 * 2**20),
    )(flat, lower_list, upper_list, base, terms, part1, part2, low1, low2, up1, up2)
    return states, pooled


def solution(mesh):
    split = P(AXES, None, None)
    in_specs = (split, P(), P(AXES, None)) + (P(),) * 9
    out_specs = (P(AXES, None, None, None), split)
    return jax.shard_map(local, mesh=mesh, in_specs=in_specs, out_specs=out_specs, check_vma=False)
```

```python
import functools
import jax
import jax.numpy as jnp
from jax import lax
from jax.experimental import pallas as pl
from jax.experimental.pallas import tpu as pltpu
from jax.sharding import PartitionSpec as P

K = 1024
D = 256
HEADS = 4
HEAD_DIM = 64
ROWS = 256
BF = jnp.bfloat16
F32 = jnp.float32


def dg(a, b, ca, cb):
    return lax.dot_general(a, b, (((ca,), (cb,)), ((), ())), preferred_element_type=F32)


def lane(shape):
    return lax.broadcasted_iota(jnp.int32, shape, 1)


def row(shape):
    return lax.broadcasted_iota(jnp.int32, shape, 0)


def project(xa, xb, ca, cb, wqk, wval, wvalt, qm, kb, vext, vtext):
    qa = dg(xa[...], wqk[...], 1, 0).astype(BF)
    kb[...] = dg(xb[...], wqk[...], 1, 0).astype(BF)
    qs = qa * jnp.asarray(HEAD_DIM**-0.5, BF)
    lanes = lane((K, D))
    for h in range(HEADS):
        inside = (lanes >= h * HEAD_DIM) & (lanes < (h + 1) * HEAD_DIM)
        qm[h] = jnp.where(inside, qs, jnp.zeros_like(qs))
    vb = dg(xb[...], wval[...], 1, 0)
    half = lane((K, 128)) < HEAD_DIM
    valid = row((K, 128)) < cb
    for h in range(HEADS):
        part = vb[:, 128 * (h // 2) : 128 * (h // 2 + 1)]
        keep = half if h % 2 == 0 else jnp.logical_not(half)
        vext[h] = jnp.where(valid, jnp.where(keep, part, 1.0), 0.0).astype(BF)
    vat = dg(wvalt[...], xa[...], 1, 1)
    validt = lane((D, K)) < ca
    vat = jnp.where(validt, vat, 0.0).astype(BF)
    ones = jnp.where(lane((HEAD_DIM, K)) < ca, 1.0, 0.0).astype(BF)
    for h in range(HEADS):
        vtext[h, :HEAD_DIM] = vat[h * HEAD_DIM : (h + 1) * HEAD_DIM]
        vtext[h, HEAD_DIM:] = ones


def attention(qm, kb, vext, vtext, e, ma, mbt):
    half = lane((ROWS, 128)) < HEAD_DIM
    for g in range(HEADS // 2):
        us = []
        for h in (2 * g, 2 * g + 1):
            slot = h % 2
            for ib in range(K // ROWS):
                rows = slice(ib * ROWS, (ib + 1) * ROWS)
                s = dg(qm[h, rows], kb[...], 1, 1)
                p = jnp.exp(s).astype(BF)
                e[slot, rows] = p
                u = dg(p, vext[h], 1, 0)
                n = u / pltpu.roll(u, HEAD_DIM, 1)
                cols = slice(128 * g, 128 * (g + 1))
                if slot == 0:
                    ma[rows, cols] = n.astype(BF)
                else:
                    ma[rows, cols] = jnp.where(half, ma[rows, cols], n.astype(BF))
            ut = dg(vtext[h], e[slot], 1, 0)
            mbt[h * HEAD_DIM : (h + 1) * HEAD_DIM] = (ut[:HEAD_DIM] / ut[HEAD_DIM:]).astype(BF)


def mlp(x, m, wout, wup, bup, gain, bias, wdown, bdown):
    sent = dg(m, wout[...], 1, 0).astype(BF)
    hidden = dg(x, wup[:D], 1, 0) + dg(sent, wup[D:], 1, 0) + bup[...]
    center = jnp.mean(hidden, axis=-1, keepdims=True)
    c = hidden - center
    spread = jnp.mean(c * c, axis=-1, keepdims=True)
    normed = c * lax.rsqrt(spread + 1e-05) * gain[...] + bias[...]
    act = (0.5 * normed * (1.0 + lax.erf(normed * 0.7071067811865476))).astype(BF)
    return dg(act, wdown[...], 1, 0) + bdown[...]


def padded(array, sides, width):
    for axis, dim in sides:
        peers, length = (lax.axis_size(axis), array.shape[dim])
        up = [(i, (i + 1) % peers) for i in range(peers - 1)]
        down = [(j, i) for i, j in up]
        last = lax.slice_in_dim(array, length - width, length, axis=dim)
        first = lax.slice_in_dim(array, 0, width, axis=dim)
        before = lax.ppermute(last, axis, up)
        after = lax.ppermute(first, axis, down)
        array = jnp.concatenate([before, array, after], axis=dim)
    return array


def shifted(array, axis, by):
    peers = lax.axis_size(axis)
    pairs = [(i, i + by) for i in range(peers) if 0 <= i + by < peers]
    return lax.ppermute(array, axis, pairs)


def attend_plain(queries, keys, values, count):
    total_rows, width = queries.shape
    heads = width // HEAD_DIM
    block = min(512, total_rows)
    key_heads = keys.reshape(keys.shape[0], heads, HEAD_DIM)
    value_heads = values.reshape(values.shape[0], heads, HEAD_DIM)
    valid = jnp.arange(keys.shape[0], dtype=jnp.int32) < count

    def one_block(query_block):
        query_heads = query_block.reshape(block, heads, HEAD_DIM)
        scores = jnp.einsum(
            "qhd,khd->hqk", query_heads, key_heads, preferred_element_type=jnp.float32
        ) * HEAD_DIM ** (-0.5)
        scores = jnp.where(valid[None, None, :], scores, -jnp.inf)
        weights = jax.nn.softmax(scores, axis=-1).astype(jnp.bfloat16)
        mixed = jnp.einsum("hqk,khd->qhd", weights, value_heads, preferred_element_type=jnp.float32)
        return mixed.reshape(block, width).astype(jnp.bfloat16)

    blocks = lax.map(one_block, queries.reshape(total_rows // block, block, width))
    return blocks.reshape(total_rows, width)


def refine(start, message, w_out, w_up, b_up, ln_gain, ln_bias, w_down, b_down):
    sent = jnp.dot(message, w_out, preferred_element_type=jnp.float32).astype(jnp.bfloat16)
    joined = jnp.concatenate([start, sent], axis=-1)
    hidden = jnp.dot(joined, w_up, preferred_element_type=jnp.float32) + b_up
    center = jnp.mean(hidden, axis=-1, keepdims=True)
    spread = jnp.mean((hidden - center) ** 2, axis=-1, keepdims=True)
    normed = (hidden - center) * lax.rsqrt(spread + 1e-05) * ln_gain + ln_bias
    act = jax.nn.gelu(normed, approximate=False).astype(jnp.bfloat16)
    delta = jnp.dot(act, w_down, preferred_element_type=jnp.float32) + b_down
    return ((start.astype(jnp.float32) + delta).astype(jnp.bfloat16), delta)


def accumulate(totals, slot_index, update):
    current = lax.dynamic_index_in_dim(totals, slot_index, 0, keepdims=False)
    return lax.dynamic_update_index_in_dim(totals, current + update, slot_index, 0)


def plain(
    descriptors,
    key_counts,
    pair_list,
    w_qk,
    w_value,
    w_out,
    w_up,
    b_up,
    ln_gain,
    ln_bias,
    w_down,
    b_down,
):
    images_here = descriptors.shape[0]
    slots_here = descriptors.shape[1]
    width = descriptors.shape[2]
    position = lax.axis_index(("photo", "worker"))
    base_image = (position - 1) * images_here
    nearby = padded(descriptors, ((("photo", "worker"), 0),), images_here)

    def fetch(image):
        record = lax.dynamic_index_in_dim(nearby, image - base_image, 0, keepdims=False)
        count = lax.dynamic_index_in_dim(key_counts, image, 0, keepdims=False)
        query_key = jnp.dot(record, w_qk, preferred_element_type=jnp.float32).astype(jnp.bfloat16)
        value_rows = jnp.dot(record, w_value, preferred_element_type=jnp.float32).astype(
            jnp.bfloat16
        )
        return (record, query_key, value_rows, count)

    def process(totals, pair_row):
        x_first, qk_first, val_first, count_first = fetch(pair_row[0])
        x_second, qk_second, val_second, count_second = fetch(pair_row[1])
        msg_first = attend_plain(qk_first, qk_second, val_second, count_second)
        msg_second = attend_plain(qk_second, qk_first, val_first, count_first)
        new_first, delta_first = refine(
            x_first, msg_first, w_out, w_up, b_up, ln_gain, ln_bias, w_down, b_down
        )
        new_second, delta_second = refine(
            x_second, msg_second, w_out, w_up, b_up, ln_gain, ln_bias, w_down, b_down
        )
        totals = accumulate(totals, pair_row[0] - base_image, delta_first)
        totals = accumulate(totals, pair_row[1] - base_image, delta_second)
        return (totals, jnp.stack([new_first, new_second], axis=0))

    empty_terms = jnp.zeros((3 * images_here, slots_here, width), jnp.float32)
    local_terms, pair_states = lax.scan(process, empty_terms, pair_list)
    lower_terms = local_terms[:images_here]
    middle_terms = local_terms[images_here : 2 * images_here]
    upper_terms = local_terms[2 * images_here :]
    from_upper = shifted(lower_terms.astype(jnp.bfloat16), ("photo", "worker"), -1).astype(
        lower_terms.dtype
    )
    from_lower = shifted(upper_terms.astype(jnp.bfloat16), ("photo", "worker"), 1).astype(
        upper_terms.dtype
    )
    pooled_update = middle_terms + from_upper + from_lower
    return (pair_states, pooled_update)


AXES = ("photo", "worker")
MESH = pl.DeviceIdType.MESH
PAIRS_HERE = 4
LIMIT = 480.0
TALL = 1e9


def pick(flag, a, b):
    return jnp.where(jnp.broadcast_to(flag, a.shape), a, b)


def mega(rounds, workers, plist, counts, x, wqk, wval, wvalt, wout, wup, bup, gain, bias, wdown, bdown,
         states, pooled, loud, lists, stage, near, db, far, acc, out, xb, qm, kb, vext, vtext, e, ma, mbt,
         flags, list_send, list_recv, x_send, x_recv, d_send, d_recv, f_send, f_recv, o_sem, p_sem):
    peers = 2**rounds
    me = lax.axis_index("photo") * workers + lax.axis_index("worker")

    def at(offset):
        other = (me + offset + peers) % peers
        return (other // workers, other % workers)

    def send(source, target, send_sem, recv_sem, offset):
        return pltpu.make_async_remote_copy(
            src_ref=source, dst_ref=target, send_sem=send_sem, recv_sem=recv_sem, device_id=at(offset), device_id_type=MESH
        )

    barrier = pltpu.get_barrier_semaphore()
    for offset in [1] + [-(2**r) for r in range(rounds)]:
        pl.semaphore_signal(barrier, inc=1, device_id=at(offset), device_id_type=MESH)
    pl.semaphore_wait(barrier, rounds + 1)

    list_copies = [send(plist, lists.at[1 - s], list_send.at[s], list_recv.at[1 - s], 2 * s - 1) for s in range(2)]
    for copy in list_copies:
        copy.start()
    acc[...] = jnp.zeros_like(acc)
    for copy in list_copies:
        copy.wait()

    def x_copy(s, p):
        return send(stage.at[s, p], near.at[1 - s, p], x_send.at[s, p], x_recv.at[1 - s, p], 2 * s - 1)

    def d_copy(s, p):
        return send(db.at[p], far.at[1 - s, p], d_send.at[s, p], d_recv.at[1 - s, p], 2 * s - 1)

    def serve(p, _):
        for s in range(2):
            place = jnp.clip(lists[s, 2 * p + 1] - PAIRS_HERE * me, 0, PAIRS_HERE - 1)
            stage[s, p] = x[place]
            x_copy(s, p).start()
        return 0

    lax.fori_loop(0, PAIRS_HERE, serve, 0)

    heads = jnp.where(row((D, 128)) // HEAD_DIM == lane((D, 128)), 1.0, 0.0).astype(BF)

    def survey(p, carry):
        top, tall = carry
        qk = dg(x[p], wqk[...], 1, 0).astype(BF).astype(F32)
        norms = dg((qk * qk).astype(BF), heads, 1, 0)
        val = jnp.abs(dg(x[p], wval[...], 1, 0))
        return (jnp.maximum(top, jnp.max(norms, axis=0, keepdims=True)),
                jnp.maximum(tall, jnp.max(val, axis=0, keepdims=True)))

    top, tall = lax.fori_loop(0, PAIRS_HERE, survey, (jnp.zeros((1, 128), F32), jnp.zeros((1, D), F32)))
    tall = jnp.maximum(tall[:, :128], tall[:, 128:])
    quiet = (top < LIMIT) & (tall < TALL)
    flags[0] = jnp.broadcast_to(jnp.where(quiet, 0.0, 1.0), (8, 128))

    def f_copy(r, distance):
        return send(flags.at[r], flags.at[rounds + 1 + r], f_send.at[r], f_recv.at[r], distance)

    def gather_flags(r, distance):
        f_copy(r, distance).wait()
        flags[r + 1] = jnp.maximum(flags[r], flags[rounds + 1 + r])

    for r in range(rounds - PAIRS_HERE):
        f_copy(r, 2**r).start()
        gather_flags(r, 2**r)

    weights = (wout, wup, bup, gain, bias, wdown, bdown)

    def pool(p):
        for s in range(2):
            d_copy(s, p).wait()
        targets = [plist[2 * p + 1], lists[0, 2 * p + 1], lists[1, 2 * p + 1]]

        def part(index, _):
            rows = pl.ds(pl.multiple_of(index * 64, 64), 64)
            terms = [db[p, rows].astype(F32), far[0, p, rows].astype(F32), far[1, p, rows].astype(F32)]
            for g in range(PAIRS_HERE):
                total = acc[g, rows]
                for target, term in zip(targets, terms):
                    total += pick(target == PAIRS_HERE * me + g, term, jnp.zeros_like(term))
                acc[g, rows] = total
            return 0

        lax.fori_loop(0, K // 64, part, 0)

    def out_copy(p):
        return pltpu.make_async_copy(out.at[p % 2], states.at[p], o_sem.at[p])

    def pair(p, distance):
        r = rounds - PAIRS_HERE + p
        f_copy(r, distance).start()
        for s in range(2):
            x_copy(s, p).wait()
        first, second = plist[2 * p], plist[2 * p + 1]
        ca, cb = counts[first], counts[second]
        place = second - PAIRS_HERE * me
        own = x[jnp.clip(place, 0, PAIRS_HERE - 1)]
        xb[...] = pick(place < 0, near[0, p], pick(place >= PAIRS_HERE, near[1, p], own))
        project(x.at[p], xb, ca, cb, wqk, wval, wvalt, qm, kb, vext, vtext)
        attention(qm, kb, vext, vtext, e, ma, mbt)

        @pl.when(p >= 2)
        def _():
            out_copy(p - 2).wait()

        slot = p % 2
        for ib in range(K // ROWS):
            rows = slice(ib * ROWS, (ib + 1) * ROWS)
            delta = mlp(xb[rows], mbt[:, rows].T, *weights)
            out[slot, 1, rows] = (xb[rows].astype(F32) + delta).astype(BF)
            db[p, rows] = delta.astype(BF)
        for s in range(2):
            d_copy(s, p).start()
        for ib in range(K // ROWS):
            rows = slice(ib * ROWS, (ib + 1) * ROWS)
            delta = mlp(x[p, rows], ma[rows], *weights)
            out[slot, 0, rows] = (x[p, rows].astype(F32) + delta).astype(BF)
            acc[p, rows] += delta
        out_copy(p).start()

        @pl.when(p >= 1)
        def _():
            pool(p - 1)

        gather_flags(r, distance)
        return distance * 2

    lax.fori_loop(0, PAIRS_HERE, pair, 2 ** (rounds - PAIRS_HERE))
    loud[...] = flags[rounds]
    pool(PAIRS_HERE - 1)
    last = pltpu.make_async_copy(acc, pooled, p_sem)
    last.start()
    out_copy(PAIRS_HERE - 2).wait()
    out_copy(PAIRS_HERE - 1).wait()
    last.wait()


def quick(descriptors, key_counts, pair_list, w_qk, w_value, w_out, w_up, b_up, ln_gain, ln_bias, w_down, b_down):
    peers = lax.axis_size(AXES)
    rounds = peers.bit_length() - 1
    whole = pl.BlockSpec(memory_space=pltpu.VMEM)
    smem = pl.BlockSpec(memory_space=pltpu.SMEM)
    hbm = pl.BlockSpec(memory_space=pl.ANY)
    weights = (w_qk, w_value, w_value.T, w_out, w_up, b_up[None], ln_gain[None], ln_bias[None], w_down, b_down[None])
    dma = pltpu.SemaphoreType.DMA
    n = PAIRS_HERE
    return pl.pallas_call(
        functools.partial(mega, rounds, lax.axis_size("worker")),
        out_shape=(
            jax.ShapeDtypeStruct((n, 2, K, D), BF),
            jax.ShapeDtypeStruct((n, K, D), F32),
            jax.ShapeDtypeStruct((8, 128), F32),
        ),
        in_specs=[smem, smem] + [whole] * (1 + len(weights)),
        out_specs=(hbm, hbm, whole),
        scratch_shapes=[
            pltpu.SMEM((2, 2 * n), jnp.int32),
            pltpu.VMEM((2, n, K, D), BF),
            pltpu.VMEM((2, n, K, D), BF),
            pltpu.VMEM((n, K, D), BF),
            pltpu.VMEM((2, n, K, D), BF),
            pltpu.VMEM((n, K, D), F32),
            pltpu.VMEM((2, 2, K, D), BF),
            pltpu.VMEM((K, D), BF),
            pltpu.VMEM((HEADS, K, D), BF),
            pltpu.VMEM((K, D), BF),
            pltpu.VMEM((HEADS, K, 128), BF),
            pltpu.VMEM((HEADS, 128, K), BF),
            pltpu.VMEM((2, K, K), BF),
            pltpu.VMEM((K, D), BF),
            pltpu.VMEM((D, K), BF),
            pltpu.VMEM((2 * rounds + 1, 8, 128), F32),
            dma((2,)), dma((2,)), dma((2, n)), dma((2, n)), dma((2, n)), dma((2, n)),
            dma((rounds,)), dma((rounds,)), dma((n,)), dma,
        ],
        compiler_params=pltpu.CompilerParams(vmem_limit_bytes=60 * 2**20, collective_id=0, has_side_effects=True),
        cost_estimate=pl.CostEstimate(flops=40 * 10**9, bytes_accessed=2 * 10**7, transcendentals=0),
    )(pair_list.reshape(-1), key_counts, descriptors, *weights)


def local(*args):
    states, pooled, loud = quick(*args)
    return lax.cond(jnp.max(loud) > 0.0, lambda: plain(*args), lambda: (states, pooled))


def solution(mesh):
    split = P(AXES, None, None)
    in_specs = (split, P(), P(AXES, None)) + (P(),) * 9
    out_specs = (P(AXES, None, None, None), split)
    return jax.shard_map(local, mesh=mesh, in_specs=in_specs, out_specs=out_specs, check_vma=False)
```

```python
import functools
import jax
import jax.numpy as jnp
from jax import lax
from jax.experimental import pallas as pl
from jax.experimental.pallas import tpu as pltpu
from jax.sharding import PartitionSpec as P

K = 1024
D = 256
HEADS = 4
HEAD_DIM = 64
ROWS = 256
TALL_ROWS = 512
BF = jnp.bfloat16
F32 = jnp.float32


def dg(a, b, ca, cb):
    return lax.dot_general(a, b, (((ca,), (cb,)), ((), ())), preferred_element_type=F32)


def lane(shape):
    return lax.broadcasted_iota(jnp.int32, shape, 1)


def row(shape):
    return lax.broadcasted_iota(jnp.int32, shape, 0)


def project(xa, xb, ca, cb, wqk, wval, wvalt, qm, kb, vext, vtext):
    qa = dg(xa[...], wqk[...], 1, 0).astype(BF)
    kb[...] = dg(xb[...], wqk[...], 1, 0).astype(BF)
    qs = qa * jnp.asarray(HEAD_DIM**-0.5, BF)
    lanes = lane((K, D))
    for h in range(HEADS):
        inside = (lanes >= h * HEAD_DIM) & (lanes < (h + 1) * HEAD_DIM)
        qm[h] = jnp.where(inside, qs, jnp.zeros_like(qs))
    vb = dg(xb[...], wval[...], 1, 0)
    half = lane((K, 128)) < HEAD_DIM
    valid = row((K, 128)) < cb
    for h in range(HEADS):
        part = vb[:, 128 * (h // 2) : 128 * (h // 2 + 1)]
        keep = half if h % 2 == 0 else jnp.logical_not(half)
        vext[h] = jnp.where(valid, jnp.where(keep, part, 1.0), 0.0).astype(BF)
    vat = dg(wvalt[...], xa[...], 1, 1)
    validt = lane((D, K)) < ca
    vat = jnp.where(validt, vat, 0.0).astype(BF)
    ones = jnp.where(lane((HEAD_DIM, K)) < ca, 1.0, 0.0).astype(BF)
    for h in range(HEADS):
        vtext[h, :HEAD_DIM] = vat[h * HEAD_DIM : (h + 1) * HEAD_DIM]
        vtext[h, HEAD_DIM:] = ones


def attention(qm, kb, vext, vtext, e, ma, mbt):
    blocks = K // TALL_ROWS
    half = lane((TALL_ROWS, 128)) < HEAD_DIM
    steps = [(h, slice(ib * TALL_ROWS, (ib + 1) * TALL_ROWS)) for h in range(HEADS) for ib in range(blocks)]

    def score(step):
        h, rows = step
        return dg(qm[h, rows], kb[...], 1, 1)

    def first(h, rows, p):
        cols = slice(128 * (h // 2), 128 * (h // 2 + 1))
        u = dg(p, vext[h], 1, 0)
        n = (u / pltpu.roll(u, HEAD_DIM, 1)).astype(BF)
        ma[rows, cols] = n if h % 2 == 0 else jnp.where(half, ma[rows, cols], n)

    def second(h):
        ut = dg(vtext[h], e[h % 2], 1, 0)
        mbt[h * HEAD_DIM : (h + 1) * HEAD_DIM] = (ut[:HEAD_DIM] / ut[HEAD_DIM:]).astype(BF)

    ahead = score(steps[0])
    held = None
    for t, (h, rows) in enumerate(steps):
        s = ahead
        if t + 1 < len(steps):
            ahead = score(steps[t + 1])
        p = jnp.exp(s).astype(BF)
        e[h % 2, rows] = p
        if held is not None:
            first(*held)
        held = (h, rows, p)
        if t % blocks == 0 and h > 0:
            second(h - 1)
    first(*held)
    second(HEADS - 1)


def mlp(get, put, steps, wout, wup, bup, gain, bias, wdown, bdown):
    def layer(i):
        x, m = get(i)
        sent = dg(m, wout[...], 1, 0).astype(BF)
        return dg(jnp.concatenate([x, sent], axis=1), wup[...], 1, 0) + bup[...]

    ahead = layer(0)
    for i in range(steps):
        hidden = ahead
        if i + 1 < steps:
            ahead = layer(i + 1)
        c = hidden - jnp.mean(hidden, axis=-1, keepdims=True)
        spread = jnp.mean(c * c, axis=-1, keepdims=True)
        normed = c * lax.rsqrt(spread + 1e-05) * gain[...] + bias[...]
        half = 0.5 * normed
        act = (half * lax.erf(normed * 0.7071067811865476) + half).astype(BF)
        put(i, dg(act, wdown[...], 1, 0) + bdown[...])


def padded(array, sides, width):
    for axis, dim in sides:
        peers, length = (lax.axis_size(axis), array.shape[dim])
        up = [(i, (i + 1) % peers) for i in range(peers - 1)]
        down = [(j, i) for i, j in up]
        last = lax.slice_in_dim(array, length - width, length, axis=dim)
        first = lax.slice_in_dim(array, 0, width, axis=dim)
        before = lax.ppermute(last, axis, up)
        after = lax.ppermute(first, axis, down)
        array = jnp.concatenate([before, array, after], axis=dim)
    return array


def shifted(array, axis, by):
    peers = lax.axis_size(axis)
    pairs = [(i, i + by) for i in range(peers) if 0 <= i + by < peers]
    return lax.ppermute(array, axis, pairs)


def attend_plain(queries, keys, values, count):
    total_rows, width = queries.shape
    heads = width // HEAD_DIM
    block = min(512, total_rows)
    key_heads = keys.reshape(keys.shape[0], heads, HEAD_DIM)
    value_heads = values.reshape(values.shape[0], heads, HEAD_DIM)
    valid = jnp.arange(keys.shape[0], dtype=jnp.int32) < count

    def one_block(query_block):
        query_heads = query_block.reshape(block, heads, HEAD_DIM)
        scores = jnp.einsum(
            "qhd,khd->hqk", query_heads, key_heads, preferred_element_type=jnp.float32
        ) * HEAD_DIM ** (-0.5)
        scores = jnp.where(valid[None, None, :], scores, -jnp.inf)
        weights = jax.nn.softmax(scores, axis=-1).astype(jnp.bfloat16)
        mixed = jnp.einsum("hqk,khd->qhd", weights, value_heads, preferred_element_type=jnp.float32)
        return mixed.reshape(block, width).astype(jnp.bfloat16)

    blocks = lax.map(one_block, queries.reshape(total_rows // block, block, width))
    return blocks.reshape(total_rows, width)


def refine(start, message, w_out, w_up, b_up, ln_gain, ln_bias, w_down, b_down):
    sent = jnp.dot(message, w_out, preferred_element_type=jnp.float32).astype(jnp.bfloat16)
    joined = jnp.concatenate([start, sent], axis=-1)
    hidden = jnp.dot(joined, w_up, preferred_element_type=jnp.float32) + b_up
    center = jnp.mean(hidden, axis=-1, keepdims=True)
    spread = jnp.mean((hidden - center) ** 2, axis=-1, keepdims=True)
    normed = (hidden - center) * lax.rsqrt(spread + 1e-05) * ln_gain + ln_bias
    act = jax.nn.gelu(normed, approximate=False).astype(jnp.bfloat16)
    delta = jnp.dot(act, w_down, preferred_element_type=jnp.float32) + b_down
    return ((start.astype(jnp.float32) + delta).astype(jnp.bfloat16), delta)


def accumulate(totals, slot_index, update):
    current = lax.dynamic_index_in_dim(totals, slot_index, 0, keepdims=False)
    return lax.dynamic_update_index_in_dim(totals, current + update, slot_index, 0)


def plain(
    descriptors,
    key_counts,
    pair_list,
    w_qk,
    w_value,
    w_out,
    w_up,
    b_up,
    ln_gain,
    ln_bias,
    w_down,
    b_down,
):
    images_here = descriptors.shape[0]
    slots_here = descriptors.shape[1]
    width = descriptors.shape[2]
    position = lax.axis_index(("photo", "worker"))
    base_image = (position - 1) * images_here
    nearby = padded(descriptors, ((("photo", "worker"), 0),), images_here)

    def fetch(image):
        record = lax.dynamic_index_in_dim(nearby, image - base_image, 0, keepdims=False)
        count = lax.dynamic_index_in_dim(key_counts, image, 0, keepdims=False)
        query_key = jnp.dot(record, w_qk, preferred_element_type=jnp.float32).astype(jnp.bfloat16)
        value_rows = jnp.dot(record, w_value, preferred_element_type=jnp.float32).astype(
            jnp.bfloat16
        )
        return (record, query_key, value_rows, count)

    def process(totals, pair_row):
        x_first, qk_first, val_first, count_first = fetch(pair_row[0])
        x_second, qk_second, val_second, count_second = fetch(pair_row[1])
        msg_first = attend_plain(qk_first, qk_second, val_second, count_second)
        msg_second = attend_plain(qk_second, qk_first, val_first, count_first)
        new_first, delta_first = refine(
            x_first, msg_first, w_out, w_up, b_up, ln_gain, ln_bias, w_down, b_down
        )
        new_second, delta_second = refine(
            x_second, msg_second, w_out, w_up, b_up, ln_gain, ln_bias, w_down, b_down
        )
        totals = accumulate(totals, pair_row[0] - base_image, delta_first)
        totals = accumulate(totals, pair_row[1] - base_image, delta_second)
        return (totals, jnp.stack([new_first, new_second], axis=0))

    empty_terms = jnp.zeros((3 * images_here, slots_here, width), jnp.float32)
    local_terms, pair_states = lax.scan(process, empty_terms, pair_list)
    lower_terms = local_terms[:images_here]
    middle_terms = local_terms[images_here : 2 * images_here]
    upper_terms = local_terms[2 * images_here :]
    from_upper = shifted(lower_terms.astype(jnp.bfloat16), ("photo", "worker"), -1).astype(
        lower_terms.dtype
    )
    from_lower = shifted(upper_terms.astype(jnp.bfloat16), ("photo", "worker"), 1).astype(
        upper_terms.dtype
    )
    pooled_update = middle_terms + from_upper + from_lower
    return (pair_states, pooled_update)


AXES = ("photo", "worker")
MESH = pl.DeviceIdType.MESH
PAIRS_HERE = 4
LIMIT = 480.0
TALL = 1e9


def pick(flag, a, b):
    return jnp.where(jnp.broadcast_to(flag, a.shape), a, b)


def mega(rounds, workers, plist, counts, descriptors, wqk, wval, wout, wup, bup, gain, bias, wdown, bdown,
         states, pooled, loud, x, wvalt, lists, stage, near, db, far, acc, out, xb, qm, kb, vext, vtext, e, ma, mbt,
         flags, list_send, list_recv, x_send, x_recv, d_send, d_recv, f_send, f_recv, o_sem, p_sem, x_sem):
    peers = 2**rounds
    me = lax.axis_index("photo") * workers + lax.axis_index("worker")

    def at(offset):
        other = (me + offset + peers) % peers
        return (other // workers, other % workers)

    def send(source, target, send_sem, recv_sem, offset):
        return pltpu.make_async_remote_copy(
            src_ref=source, dst_ref=target, send_sem=send_sem, recv_sem=recv_sem, device_id=at(offset), device_id_type=MESH
        )

    load = pltpu.make_async_copy(descriptors, x, x_sem)
    load.start()
    barrier = pltpu.get_barrier_semaphore()
    for offset in [1] + [-(2**r) for r in range(rounds)]:
        pl.semaphore_signal(barrier, inc=1, device_id=at(offset), device_id_type=MESH)
    pl.semaphore_wait(barrier, rounds + 1)

    list_copies = [send(plist, lists.at[1 - s], list_send.at[s], list_recv.at[1 - s], 2 * s - 1) for s in range(2)]
    for copy in list_copies:
        copy.start()
    acc[...] = jnp.zeros_like(acc)
    wvalt[...] = wval[...].T
    load.wait()
    for copy in list_copies:
        copy.wait()

    def x_copy(s, p):
        return send(stage.at[s, p], near.at[1 - s, p], x_send.at[s, p], x_recv.at[1 - s, p], 2 * s - 1)

    def d_copy(s, p):
        return send(db.at[p], far.at[1 - s, p], d_send.at[s, p], d_recv.at[1 - s, p], 2 * s - 1)

    def serve(p, _):
        for s in range(2):
            place = jnp.clip(lists[s, 1, p] - PAIRS_HERE * me, 0, PAIRS_HERE - 1)
            stage[s, p] = x[place]

            @pl.when(p == 0)
            def _():
                x_copy(s, p).start()

        return 0

    lax.fori_loop(0, PAIRS_HERE, serve, 0)

    heads = jnp.where(row((D, 128)) // HEAD_DIM == lane((D, 128)), 1.0, 0.0).astype(BF)

    def survey(p, carry):
        top, tall = carry
        qk = dg(x[p], wqk[...], 1, 0).astype(BF).astype(F32)
        norms = dg((qk * qk).astype(BF), heads, 1, 0)
        val = jnp.abs(dg(x[p], wval[...], 1, 0))
        return (jnp.maximum(top, jnp.max(norms, axis=0, keepdims=True)),
                jnp.maximum(tall, jnp.max(val, axis=0, keepdims=True)))

    top, tall = lax.fori_loop(0, PAIRS_HERE, survey, (jnp.zeros((1, 128), F32), jnp.zeros((1, D), F32)))
    tall = jnp.maximum(tall[:, :128], tall[:, 128:])
    quiet = (top < LIMIT) & (tall < TALL)
    flags[0] = jnp.broadcast_to(jnp.where(quiet, 0.0, 1.0), (8, 128))

    def f_copy(r, distance):
        return send(flags.at[r], flags.at[rounds + 1 + r], f_send.at[r], f_recv.at[r], distance)

    def gather_flags(r, distance):
        f_copy(r, distance).wait()
        flags[r + 1] = jnp.maximum(flags[r], flags[rounds + 1 + r])

    for r in range(rounds - PAIRS_HERE):
        f_copy(r, 2**r).start()
        gather_flags(r, 2**r)

    weights = (wout, wup, bup, gain, bias, wdown, bdown)

    def pool(p):
        for s in range(2):
            d_copy(s, p).wait()
        targets = [plist[1, p], lists[0, 1, p], lists[1, 1, p]]

        def part(index, _):
            rows = pl.ds(pl.multiple_of(index * 64, 64), 64)
            terms = [db[p, rows].astype(F32), far[0, p, rows].astype(F32), far[1, p, rows].astype(F32)]
            for g in range(PAIRS_HERE):
                total = acc[g, rows]
                for target, term in zip(targets, terms):
                    total += pick(target == PAIRS_HERE * me + g, term, jnp.zeros_like(term))
                acc[g, rows] = total
            return 0

        lax.fori_loop(0, K // 64, part, 0)

    def out_copy(p):
        return pltpu.make_async_copy(out.at[p % 2], states.at[p], o_sem.at[p])

    def pair(p, distance):
        r = rounds - PAIRS_HERE + p
        f_copy(r, distance).start()
        for s in range(2):
            x_copy(s, p).wait()

        @pl.when(p + 1 < PAIRS_HERE)
        def _():
            for s in range(2):
                x_copy(s, p + 1).start()

        first, second = plist[0, p], plist[1, p]
        ca, cb = counts[first], counts[second]
        place = second - PAIRS_HERE * me
        own = x[jnp.clip(place, 0, PAIRS_HERE - 1)]
        xb[...] = pick(place < 0, near[0, p], pick(place >= PAIRS_HERE, near[1, p], own))
        project(x.at[p], xb, ca, cb, wqk, wval, wvalt, qm, kb, vext, vtext)
        attention(qm, kb, vext, vtext, e, ma, mbt)

        @pl.when(p >= 2)
        def _():
            out_copy(p - 2).wait()

        slot = p % 2
        blocks = K // ROWS

        def get(i):
            rows = slice(i % blocks * ROWS, (i % blocks + 1) * ROWS)
            return (xb[rows], mbt[:, rows].T) if i < blocks else (x[p, rows], ma[rows])

        def put(i, delta):
            rows = slice(i % blocks * ROWS, (i % blocks + 1) * ROWS)
            if i < blocks:
                out[slot, 1, rows] = (xb[rows].astype(F32) + delta).astype(BF)
                db[p, rows] = delta.astype(BF)
            else:
                out[slot, 0, rows] = (x[p, rows].astype(F32) + delta).astype(BF)
                acc[p, rows] += delta
            if i == blocks - 1:
                for s in range(2):
                    d_copy(s, p).start()

        mlp(get, put, 2 * blocks, *weights)
        out_copy(p).start()

        @pl.when(p >= 1)
        def _():
            pool(p - 1)

        gather_flags(r, distance)
        return distance * 2

    lax.fori_loop(0, PAIRS_HERE, pair, 2 ** (rounds - PAIRS_HERE))
    loud[0] = jnp.max(flags[rounds]).astype(jnp.int32)
    pool(PAIRS_HERE - 1)
    last = pltpu.make_async_copy(acc, pooled, p_sem)
    last.start()
    out_copy(PAIRS_HERE - 2).wait()
    out_copy(PAIRS_HERE - 1).wait()
    last.wait()


def quick(descriptors, key_counts, pair_list, w_qk, w_value, w_out, w_up, b_up, ln_gain, ln_bias, w_down, b_down):
    peers = lax.axis_size(AXES)
    rounds = peers.bit_length() - 1
    whole = pl.BlockSpec(memory_space=pltpu.VMEM)
    smem = pl.BlockSpec(memory_space=pltpu.SMEM)
    hbm = pl.BlockSpec(memory_space=pl.ANY)
    weights = (w_qk, w_value, w_out, w_up, b_up[None], ln_gain[None], ln_bias[None], w_down, b_down[None])
    dma = pltpu.SemaphoreType.DMA
    n = PAIRS_HERE
    return pl.pallas_call(
        functools.partial(mega, rounds, lax.axis_size("worker")),
        out_shape=(
            jax.ShapeDtypeStruct((n, 2, K, D), BF),
            jax.ShapeDtypeStruct((n, K, D), F32),
            jax.ShapeDtypeStruct((1,), jnp.int32),
        ),
        in_specs=[smem, smem, hbm] + [whole] * len(weights),
        out_specs=(hbm, hbm, smem),
        scratch_shapes=[
            pltpu.VMEM((n, K, D), BF),
            pltpu.VMEM((D, D), BF),
            pltpu.SMEM((2, 2, n), jnp.int32),
            pltpu.VMEM((2, n, K, D), BF),
            pltpu.VMEM((2, n, K, D), BF),
            pltpu.VMEM((n, K, D), BF),
            pltpu.VMEM((2, n, K, D), BF),
            pltpu.VMEM((n, K, D), F32),
            pltpu.VMEM((2, 2, K, D), BF),
            pltpu.VMEM((K, D), BF),
            pltpu.VMEM((HEADS, K, D), BF),
            pltpu.VMEM((K, D), BF),
            pltpu.VMEM((HEADS, K, 128), BF),
            pltpu.VMEM((HEADS, 128, K), BF),
            pltpu.VMEM((2, K, K), BF),
            pltpu.VMEM((K, D), BF),
            pltpu.VMEM((D, K), BF),
            pltpu.VMEM((2 * rounds + 1, 8, 128), F32),
            dma((2,)), dma((2,)), dma((2, n)), dma((2, n)), dma((2, n)), dma((2, n)),
            dma((rounds,)), dma((rounds,)), dma((n,)), dma, dma,
        ],
        compiler_params=pltpu.CompilerParams(vmem_limit_bytes=60 * 2**20, collective_id=0, has_side_effects=True),
        cost_estimate=pl.CostEstimate(flops=40 * 10**9, bytes_accessed=2 * 10**7, transcendentals=0),
    )(pair_list.T, key_counts, descriptors, *weights)


def local(*args):
    states, pooled, loud = quick(*args)
    return lax.cond(loud[0] > 0, lambda: plain(*args), lambda: (states, pooled))


def solution(mesh):
    split = P(AXES, None, None)
    in_specs = (split, P(), P(AXES, None)) + (P(),) * 9
    out_specs = (P(AXES, None, None, None), split)
    return jax.shard_map(local, mesh=mesh, in_specs=in_specs, out_specs=out_specs, check_vma=False)
```

```python
import functools
import jax
import jax.numpy as jnp
from jax import lax
from jax.experimental import pallas as pl
from jax.experimental.pallas import tpu as pltpu
from jax.sharding import PartitionSpec as P

K = 1024
D = 256
HEADS = 4
HEAD_DIM = 64
ROWS = 256
TALL_ROWS = 512
BF = jnp.bfloat16
F32 = jnp.float32


def dg(a, b, ca, cb):
    return lax.dot_general(a, b, (((ca,), (cb,)), ((), ())), preferred_element_type=F32)


def lane(shape):
    return lax.broadcasted_iota(jnp.int32, shape, 1)


def row(shape):
    return lax.broadcasted_iota(jnp.int32, shape, 0)


def project(xb, ca, cb, wqk, wval, qa, vat, qm, kb, vext, vtext):
    kb[...] = dg(xb[...], wqk[...], 1, 0).astype(BF)
    qs = qa * jnp.asarray(HEAD_DIM**-0.5, BF)
    lanes = lane((K, D))
    for h in range(HEADS):
        inside = (lanes >= h * HEAD_DIM) & (lanes < (h + 1) * HEAD_DIM)
        qm[h] = jnp.where(inside, qs, jnp.zeros_like(qs))
    vb = dg(xb[...], wval[...], 1, 0)
    half = lane((K, 128)) < HEAD_DIM
    valid = row((K, 128)) < cb
    for h in range(HEADS):
        part = vb[:, 128 * (h // 2) : 128 * (h // 2 + 1)]
        keep = half if h % 2 == 0 else jnp.logical_not(half)
        vext[h] = jnp.where(valid, jnp.where(keep, part, 1.0), 0.0).astype(BF)
    kept = jnp.where(lane((D, K)) < ca, vat, jnp.zeros_like(vat))
    ones = jnp.where(lane((HEAD_DIM, K)) < ca, 1.0, 0.0).astype(BF)
    for h in range(HEADS):
        vtext[h, :HEAD_DIM] = kept[h * HEAD_DIM : (h + 1) * HEAD_DIM]
        vtext[h, HEAD_DIM:] = ones


def attention(qm, kb, vext, vtext, e, ma, mbt):
    blocks = K // TALL_ROWS
    half = lane((TALL_ROWS, 128)) < HEAD_DIM
    steps = [(h, slice(ib * TALL_ROWS, (ib + 1) * TALL_ROWS)) for h in range(HEADS) for ib in range(blocks)]

    def score(step):
        h, rows = step
        return dg(qm[h, rows], kb[...], 1, 1)

    def first(h, rows, p):
        cols = slice(128 * (h // 2), 128 * (h // 2 + 1))
        u = dg(p, vext[h], 1, 0)
        n = (u / pltpu.roll(u, HEAD_DIM, 1)).astype(BF)
        ma[rows, cols] = n if h % 2 == 0 else jnp.where(half, ma[rows, cols], n)

    def second(h):
        ut = dg(vtext[h], e[h % 2], 1, 0)
        mbt[h * HEAD_DIM : (h + 1) * HEAD_DIM] = (ut[:HEAD_DIM] / ut[HEAD_DIM:]).astype(BF)

    ahead = score(steps[0])
    held = None
    for t, (h, rows) in enumerate(steps):
        s = ahead
        if t + 1 < len(steps):
            ahead = score(steps[t + 1])
        p = jnp.exp(s).astype(BF)
        e[h % 2, rows] = p
        if held is not None:
            first(*held)
        held = (h, rows, p)
        if t % blocks == 0 and h > 0:
            second(h - 1)
    first(*held)
    second(HEADS - 1)


def mlp(get, put, steps, wout, wup, bup, gain, bias, wdown, bdown):
    def layer(i):
        x, m = get(i)
        sent = dg(m, wout[...], 1, 0).astype(BF)
        return dg(jnp.concatenate([x, sent], axis=1), wup[...], 1, 0) + bup[...]

    ahead = layer(0)
    for i in range(steps):
        hidden = ahead
        if i + 1 < steps:
            ahead = layer(i + 1)
        c = hidden - jnp.mean(hidden, axis=-1, keepdims=True)
        spread = jnp.mean(c * c, axis=-1, keepdims=True)
        normed = c * lax.rsqrt(spread + 1e-05) * gain[...] + bias[...]
        half = 0.5 * normed
        act = (half * lax.erf(normed * 0.7071067811865476) + half).astype(BF)
        put(i, dg(act, wdown[...], 1, 0) + bdown[...])


def padded(array, sides, width):
    for axis, dim in sides:
        peers, length = (lax.axis_size(axis), array.shape[dim])
        up = [(i, (i + 1) % peers) for i in range(peers - 1)]
        down = [(j, i) for i, j in up]
        last = lax.slice_in_dim(array, length - width, length, axis=dim)
        first = lax.slice_in_dim(array, 0, width, axis=dim)
        before = lax.ppermute(last, axis, up)
        after = lax.ppermute(first, axis, down)
        array = jnp.concatenate([before, array, after], axis=dim)
    return array


def shifted(array, axis, by):
    peers = lax.axis_size(axis)
    pairs = [(i, i + by) for i in range(peers) if 0 <= i + by < peers]
    return lax.ppermute(array, axis, pairs)


def attend_plain(queries, keys, values, count):
    total_rows, width = queries.shape
    heads = width // HEAD_DIM
    block = min(512, total_rows)
    key_heads = keys.reshape(keys.shape[0], heads, HEAD_DIM)
    value_heads = values.reshape(values.shape[0], heads, HEAD_DIM)
    valid = jnp.arange(keys.shape[0], dtype=jnp.int32) < count

    def one_block(query_block):
        query_heads = query_block.reshape(block, heads, HEAD_DIM)
        scores = jnp.einsum(
            "qhd,khd->hqk", query_heads, key_heads, preferred_element_type=jnp.float32
        ) * HEAD_DIM ** (-0.5)
        scores = jnp.where(valid[None, None, :], scores, -jnp.inf)
        weights = jax.nn.softmax(scores, axis=-1).astype(jnp.bfloat16)
        mixed = jnp.einsum("hqk,khd->qhd", weights, value_heads, preferred_element_type=jnp.float32)
        return mixed.reshape(block, width).astype(jnp.bfloat16)

    blocks = lax.map(one_block, queries.reshape(total_rows // block, block, width))
    return blocks.reshape(total_rows, width)


def refine(start, message, w_out, w_up, b_up, ln_gain, ln_bias, w_down, b_down):
    sent = jnp.dot(message, w_out, preferred_element_type=jnp.float32).astype(jnp.bfloat16)
    joined = jnp.concatenate([start, sent], axis=-1)
    hidden = jnp.dot(joined, w_up, preferred_element_type=jnp.float32) + b_up
    center = jnp.mean(hidden, axis=-1, keepdims=True)
    spread = jnp.mean((hidden - center) ** 2, axis=-1, keepdims=True)
    normed = (hidden - center) * lax.rsqrt(spread + 1e-05) * ln_gain + ln_bias
    act = jax.nn.gelu(normed, approximate=False).astype(jnp.bfloat16)
    delta = jnp.dot(act, w_down, preferred_element_type=jnp.float32) + b_down
    return ((start.astype(jnp.float32) + delta).astype(jnp.bfloat16), delta)


def accumulate(totals, slot_index, update):
    current = lax.dynamic_index_in_dim(totals, slot_index, 0, keepdims=False)
    return lax.dynamic_update_index_in_dim(totals, current + update, slot_index, 0)


def plain(
    descriptors,
    key_counts,
    pair_list,
    w_qk,
    w_value,
    w_out,
    w_up,
    b_up,
    ln_gain,
    ln_bias,
    w_down,
    b_down,
):
    images_here = descriptors.shape[0]
    slots_here = descriptors.shape[1]
    width = descriptors.shape[2]
    position = lax.axis_index(("photo", "worker"))
    base_image = (position - 1) * images_here
    nearby = padded(descriptors, ((("photo", "worker"), 0),), images_here)

    def fetch(image):
        record = lax.dynamic_index_in_dim(nearby, image - base_image, 0, keepdims=False)
        count = lax.dynamic_index_in_dim(key_counts, image, 0, keepdims=False)
        query_key = jnp.dot(record, w_qk, preferred_element_type=jnp.float32).astype(jnp.bfloat16)
        value_rows = jnp.dot(record, w_value, preferred_element_type=jnp.float32).astype(
            jnp.bfloat16
        )
        return (record, query_key, value_rows, count)

    def process(totals, pair_row):
        x_first, qk_first, val_first, count_first = fetch(pair_row[0])
        x_second, qk_second, val_second, count_second = fetch(pair_row[1])
        msg_first = attend_plain(qk_first, qk_second, val_second, count_second)
        msg_second = attend_plain(qk_second, qk_first, val_first, count_first)
        new_first, delta_first = refine(
            x_first, msg_first, w_out, w_up, b_up, ln_gain, ln_bias, w_down, b_down
        )
        new_second, delta_second = refine(
            x_second, msg_second, w_out, w_up, b_up, ln_gain, ln_bias, w_down, b_down
        )
        totals = accumulate(totals, pair_row[0] - base_image, delta_first)
        totals = accumulate(totals, pair_row[1] - base_image, delta_second)
        return (totals, jnp.stack([new_first, new_second], axis=0))

    empty_terms = jnp.zeros((3 * images_here, slots_here, width), jnp.float32)
    local_terms, pair_states = lax.scan(process, empty_terms, pair_list)
    lower_terms = local_terms[:images_here]
    middle_terms = local_terms[images_here : 2 * images_here]
    upper_terms = local_terms[2 * images_here :]
    from_upper = shifted(lower_terms.astype(jnp.bfloat16), ("photo", "worker"), -1).astype(
        lower_terms.dtype
    )
    from_lower = shifted(upper_terms.astype(jnp.bfloat16), ("photo", "worker"), 1).astype(
        upper_terms.dtype
    )
    pooled_update = middle_terms + from_upper + from_lower
    return (pair_states, pooled_update)


AXES = ("photo", "worker")
MESH = pl.DeviceIdType.MESH
PAIRS_HERE = 4
RADIX = 4
LIMIT = 480.0
TALL = 1e9


def strides(peers):
    return [peers // RADIX ** (r + 1) if peers >= RADIX ** (r + 1) else 1 for r in range(PAIRS_HERE)]


def partners(peers):
    found = {1, peers - 1}
    for stride in strides(peers):
        found |= {-k * stride % peers for k in range(1, RADIX)}
    return sorted(found)


def pick(flag, a, b):
    return jnp.where(jnp.broadcast_to(flag, a.shape), a, b)


def mega(peers, workers, plist, counts, descriptors, wqk, wval, wout, wup, bup, gain, bias, wdown, bdown,
         states, pooled, loud, x, wvalt, qa, vat, lists, stage, near, db, far, acc, out, xb, qm, kb, vext, vtext, e, ma, mbt,
         flags, heard, list_send, list_recv, x_send, x_recv, d_send, d_recv, f_send, f_recv, o_sem, p_sem, x_sem):
    me = lax.axis_index("photo") * workers + lax.axis_index("worker")

    def at(offset):
        other = (me + offset + peers) % peers
        return (other // workers, other % workers)

    def send(source, target, send_sem, recv_sem, offset):
        return pltpu.make_async_remote_copy(
            src_ref=source, dst_ref=target, send_sem=send_sem, recv_sem=recv_sem, device_id=at(offset), device_id_type=MESH
        )

    load = pltpu.make_async_copy(descriptors, x, x_sem)
    load.start()
    for s, missing in ((0, me == 0), (1, me == peers - 1)):

        @pl.when(missing)
        def _():
            for p in range(PAIRS_HERE):
                lists[s, 1, p] = -1

    barrier = pltpu.get_barrier_semaphore()
    for offset in partners(peers):
        pl.semaphore_signal(barrier, inc=1, device_id=at(offset), device_id_type=MESH)
    pl.semaphore_wait(barrier, len(partners(peers)))

    there = (me > 0, me < peers - 1)

    def each(make, act):
        for s in range(2):

            @pl.when(there[s])
            def _():
                act(make(s))

    def landed(make):
        for s in range(2):

            @pl.when(there[1 - s])
            def _():
                make(s).wait_recv()

    def list_copy(s):
        return send(plist, lists.at[1 - s], list_send.at[s], list_recv.at[1 - s], 2 * s - 1)

    def x_copy(s, p):
        return send(stage.at[s, p], near.at[1 - s, p], x_send.at[s, p], x_recv.at[1 - s, p], 2 * s - 1)

    def d_copy(s, p):
        return send(db.at[p], far.at[1 - s, p], d_send.at[s, p], d_recv.at[1 - s, p], 2 * s - 1)

    start, sent = (lambda copy: copy.start()), (lambda copy: copy.wait_send())
    each(list_copy, start)
    acc[...] = jnp.zeros_like(acc)
    wvalt[...] = wval[...].T
    load.wait()
    each(list_copy, sent)
    landed(list_copy)

    def serve(p, _):
        for s in range(2):
            place = jnp.clip(lists[s, 1, p] - PAIRS_HERE * me, 0, PAIRS_HERE - 1)
            stage[s, p] = x[place]

        @pl.when(p == 0)
        def _():
            each(lambda s: x_copy(s, 0), start)

        return 0

    lax.fori_loop(0, PAIRS_HERE, serve, 0)

    heads = jnp.where(row((D, 128)) // HEAD_DIM == lane((D, 128)), 1.0, 0.0).astype(BF)

    def survey(p, carry):
        top, tall = carry
        qk = dg(x[p], wqk[...], 1, 0).astype(BF)
        qa[p] = qk
        qk = qk.astype(F32)
        norms = dg((qk * qk).astype(BF), heads, 1, 0)
        val = dg(wvalt[...], x[p], 1, 1)
        vat[p] = val.astype(BF)
        return (jnp.maximum(top, jnp.max(norms, axis=0, keepdims=True)),
                jnp.maximum(tall, jnp.max(jnp.abs(val), axis=0, keepdims=True)))

    top, tall = lax.fori_loop(0, PAIRS_HERE, survey, (jnp.zeros((1, 128), F32), jnp.zeros((1, K), F32)))
    top = jnp.max(jnp.where(top < LIMIT, 0.0, 1.0))
    tall = jnp.max(jnp.where(tall < TALL, 0.0, 1.0))
    flags[0] = jnp.broadcast_to(jnp.maximum(top, tall), (8, 128))

    def f_copies(r, stride):
        return [send(flags.at[r], heard.at[r, k - 1], f_send.at[r, k - 1], f_recv.at[r, k - 1], k * stride)
                for k in range(1, RADIX)]

    def gather_flags(r, stride):
        total = flags[r]
        for k, copy in enumerate(f_copies(r, stride)):
            copy.wait()
            total = jnp.maximum(total, heard[r, k])
        flags[r + 1] = total

    for copy in f_copies(0, strides(peers)[0]):
        copy.start()
    each(lambda s: x_copy(s, 0), sent)
    for p in (1, 2):
        each(lambda s: x_copy(s, p), start)
    weights = (wout, wup, bup, gain, bias, wdown, bdown)

    def pool(p):
        each(lambda s: d_copy(s, p), sent)
        landed(lambda s: d_copy(s, p))
        targets = [plist[1, p], lists[0, 1, p], lists[1, 1, p]]

        def part(index, _):
            rows = pl.ds(pl.multiple_of(index * 64, 64), 64)
            terms = [db[p, rows].astype(F32), far[0, p, rows].astype(F32), far[1, p, rows].astype(F32)]
            for g in range(PAIRS_HERE):
                total = acc[g, rows]
                for target, term in zip(targets, terms):
                    total += pick(target == PAIRS_HERE * me + g, term, jnp.zeros_like(term))
                acc[g, rows] = total
            return 0

        lax.fori_loop(0, K // 64, part, 0)

    blocks = K // ROWS

    def out_copy(p, side):
        return pltpu.make_async_copy(out.at[p, side], states.at[p, side], o_sem.at[p, side])

    def pair(p, carried):
        distance = carried + p // (PAIRS_HERE - 1)

        @pl.when(p > 0)
        def _():
            each(lambda s: x_copy(s, p), sent)

        landed(lambda s: x_copy(s, p))

        @pl.when(p == 1)
        def _():
            each(lambda s: x_copy(s, PAIRS_HERE - 1), start)

        first, second = plist[0, p], plist[1, p]
        ca, cb = counts[first], counts[second]
        place = second - PAIRS_HERE * me
        own = x[jnp.clip(place, 0, PAIRS_HERE - 1)]
        xb[...] = pick(place < 0, near[0, p], pick(place >= PAIRS_HERE, near[1, p], own))
        project(xb, ca, cb, wqk, wval, qa[p], vat[p], qm, kb, vext, vtext)
        attention(qm, kb, vext, vtext, e, ma.at[p], mbt)

        def get(i):
            rows = slice(i * ROWS, (i + 1) * ROWS)
            return xb[rows], mbt[:, rows].T

        def put(i, delta):
            rows = slice(i * ROWS, (i + 1) * ROWS)
            db[p, rows] = delta.astype(BF)
            out[p, 1, rows] = (xb[rows].astype(F32) + delta).astype(BF)

        mlp(get, put, blocks, *weights)
        gather_flags(p, distance)

        @pl.when(p + 1 < PAIRS_HERE)
        def _():
            for copy in f_copies(p + 1, carried // RADIX + (p + 1) // (PAIRS_HERE - 1)):
                copy.start()

        each(lambda s: d_copy(s, p), start)
        out_copy(p, 1).start()
        return carried // RADIX

    lax.fori_loop(0, PAIRS_HERE, pair, strides(peers)[0])

    def owned(p, _):
        def get(i):
            rows = slice(i * ROWS, (i + 1) * ROWS)
            return x[p, rows], ma[p, rows]

        def put(i, delta):
            rows = slice(i * ROWS, (i + 1) * ROWS)
            out[p, 0, rows] = (x[p, rows].astype(F32) + delta).astype(BF)
            acc[p, rows] += delta

        mlp(get, put, blocks, *weights)
        out_copy(p, 0).start()
        return 0

    lax.fori_loop(0, PAIRS_HERE, owned, 0)
    loud[0] = jnp.max(flags[PAIRS_HERE]).astype(jnp.int32)
    lax.fori_loop(0, PAIRS_HERE, lambda p, _: pool(p) or 0, 0)
    last = pltpu.make_async_copy(acc, pooled, p_sem)
    last.start()
    for p in range(PAIRS_HERE):
        for side in range(2):
            out_copy(p, side).wait()
    last.wait()


def quick(descriptors, key_counts, pair_list, w_qk, w_value, w_out, w_up, b_up, ln_gain, ln_bias, w_down, b_down):
    peers = lax.axis_size(AXES)
    whole = pl.BlockSpec(memory_space=pltpu.VMEM)
    smem = pl.BlockSpec(memory_space=pltpu.SMEM)
    hbm = pl.BlockSpec(memory_space=pl.ANY)
    weights = (w_qk, w_value, w_out, w_up, b_up[None], ln_gain[None], ln_bias[None], w_down, b_down[None])
    dma = pltpu.SemaphoreType.DMA
    n = PAIRS_HERE
    return pl.pallas_call(
        functools.partial(mega, peers, lax.axis_size("worker")),
        out_shape=(
            jax.ShapeDtypeStruct((n, 2, K, D), BF),
            jax.ShapeDtypeStruct((n, K, D), F32),
            jax.ShapeDtypeStruct((1,), jnp.int32),
        ),
        in_specs=[smem, smem, hbm] + [whole] * len(weights),
        out_specs=(hbm, hbm, smem),
        scratch_shapes=[
            pltpu.VMEM((n, K, D), BF),
            pltpu.VMEM((D, D), BF),
            pltpu.VMEM((n, K, D), BF),
            pltpu.VMEM((n, D, K), BF),
            pltpu.SMEM((2, 2, n), jnp.int32),
            pltpu.VMEM((2, n, K, D), BF),
            pltpu.VMEM((2, n, K, D), BF),
            pltpu.VMEM((n, K, D), BF),
            pltpu.VMEM((2, n, K, D), BF),
            pltpu.VMEM((n, K, D), F32),
            pltpu.VMEM((n, 2, K, D), BF),
            pltpu.VMEM((K, D), BF),
            pltpu.VMEM((HEADS, K, D), BF),
            pltpu.VMEM((K, D), BF),
            pltpu.VMEM((HEADS, K, 128), BF),
            pltpu.VMEM((HEADS, 128, K), BF),
            pltpu.VMEM((2, K, K), BF),
            pltpu.VMEM((n, K, D), BF),
            pltpu.VMEM((D, K), BF),
            pltpu.VMEM((n + 1, 8, 128), F32),
            pltpu.VMEM((n, RADIX - 1, 8, 128), F32),
            dma((2,)), dma((2,)), dma((2, n)), dma((2, n)), dma((2, n)), dma((2, n)),
            dma((n, RADIX - 1)), dma((n, RADIX - 1)), dma((n, 2)), dma, dma,
        ],
        compiler_params=pltpu.CompilerParams(vmem_limit_bytes=60 * 2**20, collective_id=0, has_side_effects=True),
        cost_estimate=pl.CostEstimate(flops=40 * 10**9, bytes_accessed=2 * 10**7, transcendentals=0),
    )(pair_list.T, key_counts, descriptors, *weights)


def local(*args):
    states, pooled, loud = quick(*args)
    return lax.cond(loud[0] > 0, lambda: plain(*args), lambda: (states, pooled))


def solution(mesh):
    split = P(AXES, None, None)
    in_specs = (split, P(), P(AXES, None)) + (P(),) * 9
    out_specs = (P(AXES, None, None, None), split)
    return jax.shard_map(local, mesh=mesh, in_specs=in_specs, out_specs=out_specs, check_vma=False)
```

```python
import functools
import jax
import jax.numpy as jnp
from jax import lax
from jax.experimental import pallas as pl
from jax.experimental.pallas import tpu as pltpu
from jax.sharding import PartitionSpec as P

K = 1024
D = 256
HEADS = 4
HEAD_DIM = 64
ROWS = 256
TALL_ROWS = 512
BF = jnp.bfloat16
F32 = jnp.float32


def dg(a, b, ca, cb):
    return lax.dot_general(a, b, (((ca,), (cb,)), ((), ())), preferred_element_type=F32)


def lane(shape):
    return lax.broadcasted_iota(jnp.int32, shape, 1)


def row(shape):
    return lax.broadcasted_iota(jnp.int32, shape, 0)


def project(xb, ca, cb, wqk, wval, qa, vat, qm, kb, vext, vtext):
    kb[...] = dg(xb[...], wqk[...], 1, 0).astype(BF)
    qs = qa * jnp.asarray(HEAD_DIM**-0.5, BF)
    lanes = lane((K, D))
    for h in range(HEADS):
        inside = (lanes >= h * HEAD_DIM) & (lanes < (h + 1) * HEAD_DIM)
        qm[h] = jnp.where(inside, qs, jnp.zeros_like(qs))
    vb = dg(xb[...], wval[...], 1, 0)
    half = lane((K, 128)) < HEAD_DIM
    valid = row((K, 128)) < cb
    for h in range(HEADS):
        part = vb[:, 128 * (h // 2) : 128 * (h // 2 + 1)]
        keep = half if h % 2 == 0 else jnp.logical_not(half)
        vext[h] = jnp.where(valid, jnp.where(keep, part, 1.0), 0.0).astype(BF)
    kept = jnp.where(lane((D, K)) < ca, vat, jnp.zeros_like(vat))
    ones = jnp.where(lane((HEAD_DIM, K)) < ca, 1.0, 0.0).astype(BF)
    for h in range(HEADS):
        vtext[h, :HEAD_DIM] = kept[h * HEAD_DIM : (h + 1) * HEAD_DIM]
        vtext[h, HEAD_DIM:] = ones


def attention(qm, kb, vext, vtext, e, ma, mbt):
    blocks = K // TALL_ROWS
    half = lane((TALL_ROWS, 128)) < HEAD_DIM
    steps = [(h, slice(ib * TALL_ROWS, (ib + 1) * TALL_ROWS)) for h in range(HEADS) for ib in range(blocks)]

    def score(step):
        h, rows = step
        return dg(qm[h, rows], kb[...], 1, 1)

    def first(h, rows, p):
        cols = slice(128 * (h // 2), 128 * (h // 2 + 1))
        u = dg(p, vext[h], 1, 0)
        n = (u / pltpu.roll(u, HEAD_DIM, 1)).astype(BF)
        ma[rows, cols] = n if h % 2 == 0 else jnp.where(half, ma[rows, cols], n)

    def second(h):
        ut = dg(vtext[h], e[h % 2], 1, 0)
        mbt[h * HEAD_DIM : (h + 1) * HEAD_DIM] = (ut[:HEAD_DIM] / ut[HEAD_DIM:]).astype(BF)

    ahead = score(steps[0])
    held = None
    for t, (h, rows) in enumerate(steps):
        s = ahead
        if t + 1 < len(steps):
            ahead = score(steps[t + 1])
        p = jnp.exp(s).astype(BF)
        e[h % 2, rows] = p
        if held is not None:
            first(*held)
        held = (h, rows, p)
        if t % blocks == 0 and h > 0:
            second(h - 1)
    first(*held)
    second(HEADS - 1)


def mlp(get, put, steps, wout, wup, bup, gain, bias, wdown, bdown):
    def layer(i):
        x, m = get(i)
        sent = dg(m, wout[...], 1, 0).astype(BF)
        return dg(jnp.concatenate([x, sent], axis=1), wup[...], 1, 0) + bup[...]

    ahead = layer(0)
    for i in range(steps):
        hidden = ahead
        if i + 1 < steps:
            ahead = layer(i + 1)
        spread = jnp.mean(hidden * hidden, axis=-1, keepdims=True)
        normed = hidden * lax.rsqrt(spread + 1e-05) * gain[...] + bias[...]
        half = 0.5 * normed
        act = (half * lax.erf(normed * 0.7071067811865476) + half).astype(BF)
        put(i, dg(act, wdown[...], 1, 0) + bdown[...])


def padded(array, sides, width):
    for axis, dim in sides:
        peers, length = (lax.axis_size(axis), array.shape[dim])
        up = [(i, (i + 1) % peers) for i in range(peers - 1)]
        down = [(j, i) for i, j in up]
        last = lax.slice_in_dim(array, length - width, length, axis=dim)
        first = lax.slice_in_dim(array, 0, width, axis=dim)
        before = lax.ppermute(last, axis, up)
        after = lax.ppermute(first, axis, down)
        array = jnp.concatenate([before, array, after], axis=dim)
    return array


def shifted(array, axis, by):
    peers = lax.axis_size(axis)
    pairs = [(i, i + by) for i in range(peers) if 0 <= i + by < peers]
    return lax.ppermute(array, axis, pairs)


def attend_plain(queries, keys, values, count):
    total_rows, width = queries.shape
    heads = width // HEAD_DIM
    block = min(512, total_rows)
    key_heads = keys.reshape(keys.shape[0], heads, HEAD_DIM)
    value_heads = values.reshape(values.shape[0], heads, HEAD_DIM)
    valid = jnp.arange(keys.shape[0], dtype=jnp.int32) < count

    def one_block(query_block):
        query_heads = query_block.reshape(block, heads, HEAD_DIM)
        scores = jnp.einsum(
            "qhd,khd->hqk", query_heads, key_heads, preferred_element_type=jnp.float32
        ) * HEAD_DIM ** (-0.5)
        scores = jnp.where(valid[None, None, :], scores, -jnp.inf)
        weights = jax.nn.softmax(scores, axis=-1).astype(jnp.bfloat16)
        mixed = jnp.einsum("hqk,khd->qhd", weights, value_heads, preferred_element_type=jnp.float32)
        return mixed.reshape(block, width).astype(jnp.bfloat16)

    blocks = lax.map(one_block, queries.reshape(total_rows // block, block, width))
    return blocks.reshape(total_rows, width)


def refine(start, message, w_out, w_up, b_up, ln_gain, ln_bias, w_down, b_down):
    sent = jnp.dot(message, w_out, preferred_element_type=jnp.float32).astype(jnp.bfloat16)
    joined = jnp.concatenate([start, sent], axis=-1)
    hidden = jnp.dot(joined, w_up, preferred_element_type=jnp.float32) + b_up
    center = jnp.mean(hidden, axis=-1, keepdims=True)
    spread = jnp.mean((hidden - center) ** 2, axis=-1, keepdims=True)
    normed = (hidden - center) * lax.rsqrt(spread + 1e-05) * ln_gain + ln_bias
    act = jax.nn.gelu(normed, approximate=False).astype(jnp.bfloat16)
    delta = jnp.dot(act, w_down, preferred_element_type=jnp.float32) + b_down
    return ((start.astype(jnp.float32) + delta).astype(jnp.bfloat16), delta)


def accumulate(totals, slot_index, update):
    current = lax.dynamic_index_in_dim(totals, slot_index, 0, keepdims=False)
    return lax.dynamic_update_index_in_dim(totals, current + update, slot_index, 0)


def plain(
    descriptors,
    key_counts,
    pair_list,
    w_qk,
    w_value,
    w_out,
    w_up,
    b_up,
    ln_gain,
    ln_bias,
    w_down,
    b_down,
):
    images_here = descriptors.shape[0]
    slots_here = descriptors.shape[1]
    width = descriptors.shape[2]
    position = lax.axis_index(("photo", "worker"))
    base_image = (position - 1) * images_here
    nearby = padded(descriptors, ((("photo", "worker"), 0),), images_here)

    def fetch(image):
        record = lax.dynamic_index_in_dim(nearby, image - base_image, 0, keepdims=False)
        count = lax.dynamic_index_in_dim(key_counts, image, 0, keepdims=False)
        query_key = jnp.dot(record, w_qk, preferred_element_type=jnp.float32).astype(jnp.bfloat16)
        value_rows = jnp.dot(record, w_value, preferred_element_type=jnp.float32).astype(
            jnp.bfloat16
        )
        return (record, query_key, value_rows, count)

    def process(totals, pair_row):
        x_first, qk_first, val_first, count_first = fetch(pair_row[0])
        x_second, qk_second, val_second, count_second = fetch(pair_row[1])
        msg_first = attend_plain(qk_first, qk_second, val_second, count_second)
        msg_second = attend_plain(qk_second, qk_first, val_first, count_first)
        new_first, delta_first = refine(
            x_first, msg_first, w_out, w_up, b_up, ln_gain, ln_bias, w_down, b_down
        )
        new_second, delta_second = refine(
            x_second, msg_second, w_out, w_up, b_up, ln_gain, ln_bias, w_down, b_down
        )
        totals = accumulate(totals, pair_row[0] - base_image, delta_first)
        totals = accumulate(totals, pair_row[1] - base_image, delta_second)
        return (totals, jnp.stack([new_first, new_second], axis=0))

    empty_terms = jnp.zeros((3 * images_here, slots_here, width), jnp.float32)
    local_terms, pair_states = lax.scan(process, empty_terms, pair_list)
    lower_terms = local_terms[:images_here]
    middle_terms = local_terms[images_here : 2 * images_here]
    upper_terms = local_terms[2 * images_here :]
    from_upper = shifted(lower_terms.astype(jnp.bfloat16), ("photo", "worker"), -1).astype(
        lower_terms.dtype
    )
    from_lower = shifted(upper_terms.astype(jnp.bfloat16), ("photo", "worker"), 1).astype(
        upper_terms.dtype
    )
    pooled_update = middle_terms + from_upper + from_lower
    return (pair_states, pooled_update)


AXES = ("photo", "worker")
MESH = pl.DeviceIdType.MESH
PAIRS_HERE = 4
RADIX = 4
PART = 64
LIMIT = 480.0
TALL = 1e9


def strides(peers):
    return [peers // RADIX ** (r + 1) if peers >= RADIX ** (r + 1) else 1 for r in range(PAIRS_HERE)]


def partners(peers):
    found = {1, peers - 1}
    for stride in strides(peers):
        found |= {-k * stride % peers for k in range(1, RADIX)}
    return sorted(found)


def pick(flag, a, b):
    return jnp.where(jnp.broadcast_to(flag, a.shape), a, b)


def mega(peers, workers, plist, counts, descriptors, wqk, wval, wout, wup, bup, gain, bias, wdown, bdown,
         states, pooled, loud, x, wvalt, wupc, bupc, qa, vat, lists, stage, near, db, far, acc, out, xb, qm, kb, vext, vtext, e, ma, mbt,
         flags, heard, list_send, list_recv, x_send, x_recv, d_send, d_recv, f_send, f_recv, o_sem, p_sem, x_sem):
    me = lax.axis_index("photo") * workers + lax.axis_index("worker")

    def at(offset):
        other = (me + offset + peers) % peers
        return (other // workers, other % workers)

    def send(source, target, send_sem, recv_sem, offset):
        return pltpu.make_async_remote_copy(
            src_ref=source, dst_ref=target, send_sem=send_sem, recv_sem=recv_sem, device_id=at(offset), device_id_type=MESH
        )

    load = pltpu.make_async_copy(descriptors, x, x_sem)
    load.start()
    for s, missing in ((0, me == 0), (1, me == peers - 1)):

        @pl.when(missing)
        def _():
            for p in range(PAIRS_HERE):
                lists[s, 1, p] = -1
            far[s] = jnp.zeros_like(far[s])

    barrier = pltpu.get_barrier_semaphore()
    for offset in partners(peers):
        pl.semaphore_signal(barrier, inc=1, device_id=at(offset), device_id_type=MESH)
    pl.semaphore_wait(barrier, len(partners(peers)))

    there = (me > 0, me < peers - 1)

    def each(make, act):
        for s in range(2):

            @pl.when(there[s])
            def _():
                act(make(s))

    def landed(make):
        for s in range(2):

            @pl.when(there[1 - s])
            def _():
                make(s).wait_recv()

    def list_copy(s):
        return send(plist, lists.at[1 - s], list_send.at[s], list_recv.at[1 - s], 2 * s - 1)

    def x_copy(s, p):
        return send(stage.at[s, p], near.at[1 - s, p], x_send.at[s, p], x_recv.at[1 - s, p], 2 * s - 1)

    def d_copy(s, p):
        return send(db.at[p], far.at[1 - s, p], d_send.at[s, p], d_recv.at[1 - s, p], 2 * s - 1)

    start, sent = (lambda copy: copy.start()), (lambda copy: copy.wait_send())
    each(list_copy, start)
    acc[...] = jnp.zeros_like(acc)
    wvalt[...] = wval[...].T
    load.wait()
    each(list_copy, sent)
    landed(list_copy)

    def serve(p, _):
        for s in range(2):
            place = jnp.clip(lists[s, 1, p] - PAIRS_HERE * me, 0, PAIRS_HERE - 1)
            stage[s, p] = x[place]

        @pl.when(p == 0)
        def _():
            each(lambda s: x_copy(s, 0), start)

        return 0

    lax.fori_loop(0, PAIRS_HERE, serve, 0)

    heads = jnp.where(row((D, 128)) // HEAD_DIM == lane((D, 128)), 1.0, 0.0).astype(BF)

    def survey(p, carry):
        top, tall = carry
        qk = dg(x[p], wqk[...], 1, 0).astype(BF)
        qa[p] = qk
        qk = qk.astype(F32)
        norms = dg((qk * qk).astype(BF), heads, 1, 0)
        val = dg(wvalt[...], x[p], 1, 1)
        vat[p] = val.astype(BF)
        return (jnp.maximum(top, jnp.max(norms, axis=0, keepdims=True)),
                jnp.maximum(tall, jnp.max(jnp.abs(val), axis=0, keepdims=True)))

    top, tall = lax.fori_loop(0, PAIRS_HERE, survey, (jnp.zeros((1, 128), F32), jnp.zeros((1, K), F32)))
    top = jnp.max(jnp.where(top < LIMIT, 0.0, 1.0))
    tall = jnp.max(jnp.where(tall < TALL, 0.0, 1.0))
    flags[0] = jnp.broadcast_to(jnp.maximum(top, tall), (8, 128))

    def f_copies(r, stride):
        return [send(flags.at[r], heard.at[r, k - 1], f_send.at[r, k - 1], f_recv.at[r, k - 1], k * stride)
                for k in range(1, RADIX)]

    def gather_flags(r, stride):
        total = flags[r]
        for k, copy in enumerate(f_copies(r, stride)):
            copy.wait()
            total = jnp.maximum(total, heard[r, k])
        flags[r + 1] = total

    for copy in f_copies(0, strides(peers)[0]):
        copy.start()
    each(lambda s: x_copy(s, 0), sent)
    each(lambda s: x_copy(s, 1), start)
    up = wup[...].astype(F32)
    wupc[...] = (up - jnp.mean(up, axis=-1, keepdims=True)).astype(BF)
    bupc[...] = bup[...] - jnp.mean(bup[...], axis=-1, keepdims=True)
    weights = (wout, wupc, bupc, gain, bias, wdown, bdown)

    def pool(p):
        each(lambda s: d_copy(s, p), sent)
        landed(lambda s: d_copy(s, p))
        targets = [plist[1, p], lists[0, 1, p], lists[1, 1, p]]

        shape = (PAIRS_HERE * PART, 3 * PART)
        line, column = row(shape), lane(shape)
        source = column // PART
        target = jnp.where(source == 0, targets[0], jnp.where(source == 1, targets[1], targets[2]))
        chosen = (line % PART == column % PART) & (target == PAIRS_HERE * me + line // PART)
        chosen = jnp.where(chosen, 1.0, 0.0).astype(BF)
        for i in range(K // PART):
            rows = slice(i * PART, (i + 1) * PART)
            terms = jnp.concatenate([db[p, rows], far[0, p, rows], far[1, p, rows]], axis=0)
            total = dg(chosen, terms, 1, 0)
            for g in range(PAIRS_HERE):
                acc[g, rows] += total[g * PART : (g + 1) * PART]

    blocks = K // ROWS

    def out_copy(p, side):
        return pltpu.make_async_copy(out.at[p, side], states.at[p, side], o_sem.at[p, side])

    def pair(p, carried):
        distance = carried + p // (PAIRS_HERE - 1)

        @pl.when(p > 0)
        def _():
            each(lambda s: x_copy(s, p), sent)

        landed(lambda s: x_copy(s, p))

        @pl.when(p + 2 < PAIRS_HERE)
        def _():
            each(lambda s: x_copy(s, p + 2), start)

        first, second = plist[0, p], plist[1, p]
        ca, cb = counts[first], counts[second]
        place = second - PAIRS_HERE * me
        own = x[jnp.clip(place, 0, PAIRS_HERE - 1)]
        xb[...] = pick(place < 0, near[0, p], pick(place >= PAIRS_HERE, near[1, p], own))
        project(xb, ca, cb, wqk, wval, qa[p], vat[p], qm, kb, vext, vtext)
        attention(qm, kb, vext, vtext, e, ma.at[p], mbt)

        def get(i):
            rows = slice(i * ROWS, (i + 1) * ROWS)
            return xb[rows], mbt[:, rows].T

        def put(i, delta):
            rows = slice(i * ROWS, (i + 1) * ROWS)
            db[p, rows] = delta.astype(BF)
            out[p, 1, rows] = (xb[rows].astype(F32) + delta).astype(BF)

        mlp(get, put, blocks, *weights)

        @pl.when(p + 1 < PAIRS_HERE)
        def _():
            gather_flags(p, distance)
            for copy in f_copies(p + 1, carried // RADIX + (p + 1) // (PAIRS_HERE - 1)):
                copy.start()

        each(lambda s: d_copy(s, p), start)
        out_copy(p, 1).start()
        return carried // RADIX

    lax.fori_loop(0, PAIRS_HERE, pair, strides(peers)[0])

    def owned(q, _):
        def place(i):
            return 2 * q + i // blocks, slice(i % blocks * ROWS, (i % blocks + 1) * ROWS)

        def get(i):
            p, rows = place(i)
            return x[p, rows], ma[p, rows]

        def put(i, delta):
            p, rows = place(i)
            out[p, 0, rows] = (x[p, rows].astype(F32) + delta).astype(BF)
            acc[p, rows] += delta

        mlp(get, put, 2 * blocks, *weights)
        for i in range(2):
            out_copy(2 * q + i, 0).start()
        return 0

    lax.fori_loop(0, PAIRS_HERE // 2, owned, 0)
    gather_flags(PAIRS_HERE - 1, 1)
    loud[0] = jnp.max(flags[PAIRS_HERE]).astype(jnp.int32)
    lax.fori_loop(0, PAIRS_HERE, lambda p, _: pool(p) or 0, 0)
    last = pltpu.make_async_copy(acc, pooled, p_sem)
    last.start()
    for p in range(PAIRS_HERE):
        for side in range(2):
            out_copy(p, side).wait()
    last.wait()


def quick(descriptors, key_counts, pair_list, w_qk, w_value, w_out, w_up, b_up, ln_gain, ln_bias, w_down, b_down):
    peers = lax.axis_size(AXES)
    whole = pl.BlockSpec(memory_space=pltpu.VMEM)
    smem = pl.BlockSpec(memory_space=pltpu.SMEM)
    hbm = pl.BlockSpec(memory_space=pl.ANY)
    weights = (w_qk, w_value, w_out, w_up, b_up[None], ln_gain[None], ln_bias[None], w_down, b_down[None])
    dma = pltpu.SemaphoreType.DMA
    n = PAIRS_HERE
    return pl.pallas_call(
        functools.partial(mega, peers, lax.axis_size("worker")),
        out_shape=(
            jax.ShapeDtypeStruct((n, 2, K, D), BF),
            jax.ShapeDtypeStruct((n, K, D), F32),
            jax.ShapeDtypeStruct((1,), jnp.int32),
        ),
        in_specs=[smem, smem, hbm] + [whole] * len(weights),
        out_specs=(hbm, hbm, smem),
        scratch_shapes=[
            pltpu.VMEM((n, K, D), BF),
            pltpu.VMEM((D, D), BF),
            pltpu.VMEM(w_up.shape, BF),
            pltpu.VMEM((1, w_up.shape[1]), F32),
            pltpu.VMEM((n, K, D), BF),
            pltpu.VMEM((n, D, K), BF),
            pltpu.SMEM((2, 2, n), jnp.int32),
            pltpu.VMEM((2, n, K, D), BF),
            pltpu.VMEM((2, n, K, D), BF),
            pltpu.VMEM((n, K, D), BF),
            pltpu.VMEM((2, n, K, D), BF),
            pltpu.VMEM((n, K, D), F32),
            pltpu.VMEM((n, 2, K, D), BF),
            pltpu.VMEM((K, D), BF),
            pltpu.VMEM((HEADS, K, D), BF),
            pltpu.VMEM((K, D), BF),
            pltpu.VMEM((HEADS, K, 128), BF),
            pltpu.VMEM((HEADS, 128, K), BF),
            pltpu.VMEM((2, K, K), BF),
            pltpu.VMEM((n, K, D), BF),
            pltpu.VMEM((D, K), BF),
            pltpu.VMEM((n + 1, 8, 128), F32),
            pltpu.VMEM((n, RADIX - 1, 8, 128), F32),
            dma((2,)), dma((2,)), dma((2, n)), dma((2, n)), dma((2, n)), dma((2, n)),
            dma((n, RADIX - 1)), dma((n, RADIX - 1)), dma((n, 2)), dma, dma,
        ],
        compiler_params=pltpu.CompilerParams(vmem_limit_bytes=60 * 2**20, collective_id=0, has_side_effects=True),
        cost_estimate=pl.CostEstimate(flops=40 * 10**9, bytes_accessed=2 * 10**7, transcendentals=0),
    )(pair_list.T, key_counts, descriptors, *weights)


def local(*args):
    states, pooled, loud = quick(*args)
    return lax.cond(loud[0] > 0, lambda: plain(*args), lambda: (states, pooled))


def solution(mesh):
    split = P(AXES, None, None)
    in_specs = (split, P(), P(AXES, None)) + (P(),) * 9
    out_specs = (P(AXES, None, None, None), split)
    return jax.shard_map(local, mesh=mesh, in_specs=in_specs, out_specs=out_specs, check_vma=False)
```

```python
import functools
import jax
import jax.numpy as jnp
from jax import lax
from jax.experimental import pallas as pl
from jax.experimental.pallas import tpu as pltpu
from jax.sharding import PartitionSpec as P

K = 1024
D = 256
HEADS = 4
HEAD_DIM = 64
ROWS = 256
TALL_ROWS = 512
BF = jnp.bfloat16
F32 = jnp.float32


def dg(a, b, ca, cb):
    return lax.dot_general(a, b, (((ca,), (cb,)), ((), ())), preferred_element_type=F32)


def lane(shape):
    return lax.broadcasted_iota(jnp.int32, shape, 1)


def row(shape):
    return lax.broadcasted_iota(jnp.int32, shape, 0)


def project(xb, ca, cb, wqk, wval, qa, vat, qm, kb, vext, vtext):
    kb[...] = dg(xb[...], wqk[...], 1, 0).astype(BF)
    qs = qa * jnp.asarray(HEAD_DIM**-0.5, BF)
    lanes = lane((K, D))
    for h in range(HEADS):
        inside = (lanes >= h * HEAD_DIM) & (lanes < (h + 1) * HEAD_DIM)
        qm[h] = jnp.where(inside, qs, jnp.zeros_like(qs))
    vb = dg(xb[...], wval[...], 1, 0)
    half = lane((K, 128)) < HEAD_DIM
    valid = row((K, 128)) < cb
    for h in range(HEADS):
        part = vb[:, 128 * (h // 2) : 128 * (h // 2 + 1)]
        keep = half if h % 2 == 0 else jnp.logical_not(half)
        vext[h] = jnp.where(valid, jnp.where(keep, part, 1.0), 0.0).astype(BF)
    kept = jnp.where(lane((D, K)) < ca, vat, jnp.zeros_like(vat))
    ones = jnp.where(lane((HEAD_DIM, K)) < ca, 1.0, 0.0).astype(BF)
    for h in range(HEADS):
        vtext[h, :HEAD_DIM] = kept[h * HEAD_DIM : (h + 1) * HEAD_DIM]
        vtext[h, HEAD_DIM:] = ones


def attention(qm, kb, vext, vtext, e, ma, mbt):
    blocks = K // TALL_ROWS
    half = lane((TALL_ROWS, 128)) < HEAD_DIM
    steps = [(h, slice(ib * TALL_ROWS, (ib + 1) * TALL_ROWS)) for h in range(HEADS) for ib in range(blocks)]

    def score(step):
        h, rows = step
        return dg(qm[h, rows], kb[...], 1, 1)

    def first(h, rows, p):
        cols = slice(128 * (h // 2), 128 * (h // 2 + 1))
        u = dg(p, vext[h], 1, 0)
        n = (u / pltpu.roll(u, HEAD_DIM, 1)).astype(BF)
        ma[rows, cols] = n if h % 2 == 0 else jnp.where(half, ma[rows, cols], n)

    def second(h):
        ut = dg(vtext[h], e[h % 2], 1, 0)
        mbt[h * HEAD_DIM : (h + 1) * HEAD_DIM] = (ut[:HEAD_DIM] / ut[HEAD_DIM:]).astype(BF)

    ahead = score(steps[0])
    held = None
    for t, (h, rows) in enumerate(steps):
        s = ahead
        if t + 1 < len(steps):
            ahead = score(steps[t + 1])
        p = jnp.exp(s).astype(BF)
        e[h % 2, rows] = p
        if held is not None:
            first(*held)
        held = (h, rows, p)
        if t % blocks == 0 and h > 0:
            second(h - 1)
    first(*held)
    second(HEADS - 1)


def mlp(get, put, steps, wout, wup, bup, gain, bias, wdown, bdown):
    def layer(i):
        x, m = get(i)
        sent = dg(m, wout[...], 1, 0).astype(BF)
        return dg(jnp.concatenate([x, sent], axis=1), wup[...], 1, 0) + bup[...]

    ahead = layer(0)
    for i in range(steps):
        hidden = ahead
        if i + 1 < steps:
            ahead = layer(i + 1)
        spread = jnp.mean(hidden * hidden, axis=-1, keepdims=True)
        normed = hidden * lax.rsqrt(spread + 1e-05) * gain[...] + bias[...]
        half = 0.5 * normed
        act = (half * lax.erf(normed * 0.7071067811865476) + half).astype(BF)
        put(i, dg(act, wdown[...], 1, 0) + bdown[...])


def padded(array, sides, width):
    for axis, dim in sides:
        peers, length = (lax.axis_size(axis), array.shape[dim])
        up = [(i, (i + 1) % peers) for i in range(peers - 1)]
        down = [(j, i) for i, j in up]
        last = lax.slice_in_dim(array, length - width, length, axis=dim)
        first = lax.slice_in_dim(array, 0, width, axis=dim)
        before = lax.ppermute(last, axis, up)
        after = lax.ppermute(first, axis, down)
        array = jnp.concatenate([before, array, after], axis=dim)
    return array


def shifted(array, axis, by):
    peers = lax.axis_size(axis)
    pairs = [(i, i + by) for i in range(peers) if 0 <= i + by < peers]
    return lax.ppermute(array, axis, pairs)


def attend_plain(queries, keys, values, count):
    total_rows, width = queries.shape
    heads = width // HEAD_DIM
    block = min(512, total_rows)
    key_heads = keys.reshape(keys.shape[0], heads, HEAD_DIM)
    value_heads = values.reshape(values.shape[0], heads, HEAD_DIM)
    valid = jnp.arange(keys.shape[0], dtype=jnp.int32) < count

    def one_block(query_block):
        query_heads = query_block.reshape(block, heads, HEAD_DIM)
        scores = jnp.einsum(
            "qhd,khd->hqk", query_heads, key_heads, preferred_element_type=jnp.float32
        ) * HEAD_DIM ** (-0.5)
        scores = jnp.where(valid[None, None, :], scores, -jnp.inf)
        weights = jax.nn.softmax(scores, axis=-1).astype(jnp.bfloat16)
        mixed = jnp.einsum("hqk,khd->qhd", weights, value_heads, preferred_element_type=jnp.float32)
        return mixed.reshape(block, width).astype(jnp.bfloat16)

    blocks = lax.map(one_block, queries.reshape(total_rows // block, block, width))
    return blocks.reshape(total_rows, width)


def refine(start, message, w_out, w_up, b_up, ln_gain, ln_bias, w_down, b_down):
    sent = jnp.dot(message, w_out, preferred_element_type=jnp.float32).astype(jnp.bfloat16)
    joined = jnp.concatenate([start, sent], axis=-1)
    hidden = jnp.dot(joined, w_up, preferred_element_type=jnp.float32) + b_up
    center = jnp.mean(hidden, axis=-1, keepdims=True)
    spread = jnp.mean((hidden - center) ** 2, axis=-1, keepdims=True)
    normed = (hidden - center) * lax.rsqrt(spread + 1e-05) * ln_gain + ln_bias
    act = jax.nn.gelu(normed, approximate=False).astype(jnp.bfloat16)
    delta = jnp.dot(act, w_down, preferred_element_type=jnp.float32) + b_down
    return ((start.astype(jnp.float32) + delta).astype(jnp.bfloat16), delta)


def accumulate(totals, slot_index, update):
    current = lax.dynamic_index_in_dim(totals, slot_index, 0, keepdims=False)
    return lax.dynamic_update_index_in_dim(totals, current + update, slot_index, 0)


def plain(
    descriptors,
    key_counts,
    pair_list,
    w_qk,
    w_value,
    w_out,
    w_up,
    b_up,
    ln_gain,
    ln_bias,
    w_down,
    b_down,
):
    images_here = descriptors.shape[0]
    slots_here = descriptors.shape[1]
    width = descriptors.shape[2]
    position = lax.axis_index(("photo", "worker"))
    base_image = (position - 1) * images_here
    nearby = padded(descriptors, ((("photo", "worker"), 0),), images_here)

    def fetch(image):
        record = lax.dynamic_index_in_dim(nearby, image - base_image, 0, keepdims=False)
        count = lax.dynamic_index_in_dim(key_counts, image, 0, keepdims=False)
        query_key = jnp.dot(record, w_qk, preferred_element_type=jnp.float32).astype(jnp.bfloat16)
        value_rows = jnp.dot(record, w_value, preferred_element_type=jnp.float32).astype(
            jnp.bfloat16
        )
        return (record, query_key, value_rows, count)

    def process(totals, pair_row):
        x_first, qk_first, val_first, count_first = fetch(pair_row[0])
        x_second, qk_second, val_second, count_second = fetch(pair_row[1])
        msg_first = attend_plain(qk_first, qk_second, val_second, count_second)
        msg_second = attend_plain(qk_second, qk_first, val_first, count_first)
        new_first, delta_first = refine(
            x_first, msg_first, w_out, w_up, b_up, ln_gain, ln_bias, w_down, b_down
        )
        new_second, delta_second = refine(
            x_second, msg_second, w_out, w_up, b_up, ln_gain, ln_bias, w_down, b_down
        )
        totals = accumulate(totals, pair_row[0] - base_image, delta_first)
        totals = accumulate(totals, pair_row[1] - base_image, delta_second)
        return (totals, jnp.stack([new_first, new_second], axis=0))

    empty_terms = jnp.zeros((3 * images_here, slots_here, width), jnp.float32)
    local_terms, pair_states = lax.scan(process, empty_terms, pair_list)
    lower_terms = local_terms[:images_here]
    middle_terms = local_terms[images_here : 2 * images_here]
    upper_terms = local_terms[2 * images_here :]
    from_upper = shifted(lower_terms.astype(jnp.bfloat16), ("photo", "worker"), -1).astype(
        lower_terms.dtype
    )
    from_lower = shifted(upper_terms.astype(jnp.bfloat16), ("photo", "worker"), 1).astype(
        upper_terms.dtype
    )
    pooled_update = middle_terms + from_upper + from_lower
    return (pair_states, pooled_update)


AXES = ("photo", "worker")
MESH = pl.DeviceIdType.MESH
PAIRS_HERE = 4
RADIX = 4
PART = 64
FLUSH = 256
LIMIT = 480.0
TALL = 1e9


def strides(peers):
    return [peers // RADIX ** (r + 1) if peers >= RADIX ** (r + 1) else 1 for r in range(PAIRS_HERE)]


def partners(peers):
    found = {1, peers - 1}
    for stride in strides(peers):
        found |= {-k * stride % peers for k in range(1, RADIX)}
    return sorted(found)


def pick(flag, a, b):
    return jnp.where(jnp.broadcast_to(flag, a.shape), a, b)


def mega(peers, workers, plist, counts, descriptors, wqk, wval, wout, wup, bup, gain, bias, wdown, bdown,
         states, pooled, loud, x, wvalt, wupc, bupc, qa, vat, lists, stage, near, db, far, acc, out, xb, qm, kb, vext, vtext, e, ma, mbt,
         flags, heard, list_send, list_recv, x_send, x_recv, d_send, d_recv, f_send, f_recv, o_sem, p_sem, x_sem):
    me = lax.axis_index("photo") * workers + lax.axis_index("worker")

    def at(offset):
        other = (me + offset + peers) % peers
        return (other // workers, other % workers)

    def send(source, target, send_sem, recv_sem, offset):
        return pltpu.make_async_remote_copy(
            src_ref=source, dst_ref=target, send_sem=send_sem, recv_sem=recv_sem, device_id=at(offset), device_id_type=MESH
        )

    load = pltpu.make_async_copy(descriptors, x, x_sem)
    load.start()
    for s, missing in ((0, me == 0), (1, me == peers - 1)):

        @pl.when(missing)
        def _():
            for p in range(PAIRS_HERE):
                lists[s, 1, p] = -1
            far[s] = jnp.zeros_like(far[s])

    barrier = pltpu.get_barrier_semaphore()
    for offset in partners(peers):
        pl.semaphore_signal(barrier, inc=1, device_id=at(offset), device_id_type=MESH)
    pl.semaphore_wait(barrier, len(partners(peers)))

    there = (me > 0, me < peers - 1)

    def each(make, act):
        for s in range(2):

            @pl.when(there[s])
            def _():
                act(make(s))

    def landed(make):
        for s in range(2):

            @pl.when(there[1 - s])
            def _():
                make(s).wait_recv()

    def list_copy(s):
        return send(plist, lists.at[1 - s], list_send.at[s], list_recv.at[1 - s], 2 * s - 1)

    def x_copy(s, p):
        return send(stage.at[s, p], near.at[1 - s, p], x_send.at[s, p], x_recv.at[1 - s, p], 2 * s - 1)

    def d_copy(s, p):
        return send(db.at[p], far.at[1 - s, p], d_send.at[s, p], d_recv.at[1 - s, p], 2 * s - 1)

    start, sent = (lambda copy: copy.start()), (lambda copy: copy.wait_send())
    each(list_copy, start)
    acc[...] = jnp.zeros_like(acc)
    wvalt[...] = wval[...].T
    load.wait()
    each(list_copy, sent)
    landed(list_copy)

    def serve(p, _):
        for s in range(2):
            place = jnp.clip(lists[s, 1, p] - PAIRS_HERE * me, 0, PAIRS_HERE - 1)
            stage[s, p] = x[place]

        @pl.when(p == 0)
        def _():
            each(lambda s: x_copy(s, 0), start)

        return 0

    lax.fori_loop(0, PAIRS_HERE, serve, 0)

    heads = jnp.where(row((D, 128)) // HEAD_DIM == lane((D, 128)), 1.0, 0.0).astype(BF)

    def survey(p, carry):
        top, tall = carry
        qk = dg(x[p], wqk[...], 1, 0).astype(BF)
        qa[p] = qk
        qk = qk.astype(F32)
        norms = dg((qk * qk).astype(BF), heads, 1, 0)
        val = dg(wvalt[...], x[p], 1, 1)
        vat[p] = val.astype(BF)
        return (jnp.maximum(top, jnp.max(norms, axis=0, keepdims=True)),
                jnp.maximum(tall, jnp.max(jnp.abs(val), axis=0, keepdims=True)))

    top, tall = lax.fori_loop(0, PAIRS_HERE, survey, (jnp.zeros((1, 128), F32), jnp.zeros((1, K), F32)))
    top = jnp.max(jnp.where(top < LIMIT, 0.0, 1.0))
    tall = jnp.max(jnp.where(tall < TALL, 0.0, 1.0))
    flags[0] = jnp.broadcast_to(jnp.maximum(top, tall), (8, 128))

    def f_copies(r, stride):
        return [send(flags.at[r], heard.at[r, k - 1], f_send.at[r, k - 1], f_recv.at[r, k - 1], k * stride)
                for k in range(1, RADIX)]

    def gather_flags(r, stride):
        total = flags[r]
        for k, copy in enumerate(f_copies(r, stride)):
            copy.wait()
            total = jnp.maximum(total, heard[r, k])
        flags[r + 1] = total

    for copy in f_copies(0, strides(peers)[0]):
        copy.start()
    each(lambda s: x_copy(s, 0), sent)
    each(lambda s: x_copy(s, 1), start)
    up = wup[...].astype(F32)
    wupc[...] = (up - jnp.mean(up, axis=-1, keepdims=True)).astype(BF)
    bupc[...] = bup[...] - jnp.mean(bup[...], axis=-1, keepdims=True)
    weights = (wout, wupc, bupc, gain, bias, wdown, bdown)

    def pool(p, done=None):
        each(lambda s: d_copy(s, p), sent)
        landed(lambda s: d_copy(s, p))
        targets = [plist[1, p], lists[0, 1, p], lists[1, 1, p]]

        shape = (PAIRS_HERE * PART, 3 * PART)
        line, column = row(shape), lane(shape)
        source = column // PART
        target = jnp.where(source == 0, targets[0], jnp.where(source == 1, targets[1], targets[2]))
        chosen = (line % PART == column % PART) & (target == PAIRS_HERE * me + line // PART)
        chosen = jnp.where(chosen, 1.0, 0.0).astype(BF)
        for i in range(K // PART):
            rows = slice(i * PART, (i + 1) * PART)
            terms = jnp.concatenate([db[p, rows], far[0, p, rows], far[1, p, rows]], axis=0)
            total = dg(chosen, terms, 1, 0)
            for g in range(PAIRS_HERE):
                acc[g, rows] += total[g * PART : (g + 1) * PART]
            if done is not None and (i + 1) * PART % FLUSH == 0:
                done((i + 1) * PART // FLUSH - 1)

    blocks = K // ROWS

    def out_copy(p, side):
        return pltpu.make_async_copy(out.at[p, side], states.at[p, side], o_sem.at[p, side])

    def pair(p, carried):
        distance = carried + p // (PAIRS_HERE - 1)

        @pl.when(p > 0)
        def _():
            each(lambda s: x_copy(s, p), sent)

        landed(lambda s: x_copy(s, p))

        @pl.when(p + 2 < PAIRS_HERE)
        def _():
            each(lambda s: x_copy(s, p + 2), start)

        first, second = plist[0, p], plist[1, p]
        ca, cb = counts[first], counts[second]
        place = second - PAIRS_HERE * me
        own = x[jnp.clip(place, 0, PAIRS_HERE - 1)]
        xb[...] = pick(place < 0, near[0, p], pick(place >= PAIRS_HERE, near[1, p], own))
        project(xb, ca, cb, wqk, wval, qa[p], vat[p], qm, kb, vext, vtext)
        attention(qm, kb, vext, vtext, e, ma.at[p], mbt)

        def get(i):
            rows = slice(i * ROWS, (i + 1) * ROWS)
            return xb[rows], mbt[:, rows].T

        def put(i, delta):
            rows = slice(i * ROWS, (i + 1) * ROWS)
            db[p, rows] = delta.astype(BF)
            out[p, 1, rows] = (xb[rows].astype(F32) + delta).astype(BF)

        mlp(get, put, blocks, *weights)

        @pl.when(p + 1 < PAIRS_HERE)
        def _():
            gather_flags(p, distance)
            for copy in f_copies(p + 1, carried // RADIX + (p + 1) // (PAIRS_HERE - 1)):
                copy.start()

        each(lambda s: d_copy(s, p), start)
        out_copy(p, 1).start()
        return carried // RADIX

    lax.fori_loop(0, PAIRS_HERE, pair, strides(peers)[0])

    def owned(q, _):
        def place(i):
            return 2 * q + i // blocks, slice(i % blocks * ROWS, (i % blocks + 1) * ROWS)

        def get(i):
            p, rows = place(i)
            return x[p, rows], ma[p, rows]

        def put(i, delta):
            p, rows = place(i)
            out[p, 0, rows] = (x[p, rows].astype(F32) + delta).astype(BF)
            acc[p, rows] += delta

        mlp(get, put, 2 * blocks, *weights)
        for i in range(2):
            out_copy(2 * q + i, 0).start()
        return 0

    lax.fori_loop(0, PAIRS_HERE // 2, owned, 0)
    gather_flags(PAIRS_HERE - 1, 1)
    loud[0] = jnp.max(flags[PAIRS_HERE]).astype(jnp.int32)
    lax.fori_loop(0, PAIRS_HERE - 1, lambda p, _: pool(p) or 0, 0)

    def flush(i):
        rows = pl.ds(i * FLUSH, FLUSH)
        return pltpu.make_async_copy(acc.at[:, rows], pooled.at[:, rows], p_sem.at[i])

    pool(PAIRS_HERE - 1, lambda i: flush(i).start())
    for p in range(PAIRS_HERE):
        for side in range(2):
            out_copy(p, side).wait()
    for i in range(K // FLUSH):
        flush(i).wait()


def quick(descriptors, key_counts, pair_list, w_qk, w_value, w_out, w_up, b_up, ln_gain, ln_bias, w_down, b_down):
    peers = lax.axis_size(AXES)
    whole = pl.BlockSpec(memory_space=pltpu.VMEM)
    smem = pl.BlockSpec(memory_space=pltpu.SMEM)
    hbm = pl.BlockSpec(memory_space=pl.ANY)
    weights = (w_qk, w_value, w_out, w_up, b_up[None], ln_gain[None], ln_bias[None], w_down, b_down[None])
    dma = pltpu.SemaphoreType.DMA
    n = PAIRS_HERE
    return pl.pallas_call(
        functools.partial(mega, peers, lax.axis_size("worker")),
        out_shape=(
            jax.ShapeDtypeStruct((n, 2, K, D), BF),
            jax.ShapeDtypeStruct((n, K, D), F32),
            jax.ShapeDtypeStruct((1,), jnp.int32),
        ),
        in_specs=[smem, smem, hbm] + [whole] * len(weights),
        out_specs=(hbm, hbm, smem),
        scratch_shapes=[
            pltpu.VMEM((n, K, D), BF),
            pltpu.VMEM((D, D), BF),
            pltpu.VMEM(w_up.shape, BF),
            pltpu.VMEM((1, w_up.shape[1]), F32),
            pltpu.VMEM((n, K, D), BF),
            pltpu.VMEM((n, D, K), BF),
            pltpu.SMEM((2, 2, n), jnp.int32),
            pltpu.VMEM((2, n, K, D), BF),
            pltpu.VMEM((2, n, K, D), BF),
            pltpu.VMEM((n, K, D), BF),
            pltpu.VMEM((2, n, K, D), BF),
            pltpu.VMEM((n, K, D), F32),
            pltpu.VMEM((n, 2, K, D), BF),
            pltpu.VMEM((K, D), BF),
            pltpu.VMEM((HEADS, K, D), BF),
            pltpu.VMEM((K, D), BF),
            pltpu.VMEM((HEADS, K, 128), BF),
            pltpu.VMEM((HEADS, 128, K), BF),
            pltpu.VMEM((2, K, K), BF),
            pltpu.VMEM((n, K, D), BF),
            pltpu.VMEM((D, K), BF),
            pltpu.VMEM((n + 1, 8, 128), F32),
            pltpu.VMEM((n, RADIX - 1, 8, 128), F32),
            dma((2,)), dma((2,)), dma((2, n)), dma((2, n)), dma((2, n)), dma((2, n)),
            dma((n, RADIX - 1)), dma((n, RADIX - 1)), dma((n, 2)), dma((K // FLUSH,)), dma,
        ],
        compiler_params=pltpu.CompilerParams(vmem_limit_bytes=60 * 2**20, collective_id=0, has_side_effects=True),
        cost_estimate=pl.CostEstimate(flops=40 * 10**9, bytes_accessed=2 * 10**7, transcendentals=0),
    )(pair_list.T, key_counts, descriptors, *weights)


def local(*args):
    states, pooled, loud = quick(*args)
    return lax.cond(loud[0] > 0, lambda: plain(*args), lambda: (states, pooled))


def solution(mesh):
    split = P(AXES, None, None)
    in_specs = (split, P(), P(AXES, None)) + (P(),) * 9
    out_specs = (P(AXES, None, None, None), split)
    return jax.shard_map(local, mesh=mesh, in_specs=in_specs, out_specs=out_specs, check_vma=False)
```
